512 devices in a mesh: seq: 128 (over x, z, y_lo), chan: 4 (over y_hi, core).
Axes of the slice: x: 4, y: 8 (y_hi: 2, y_lo: 4; y = y_hi * 4 + y_lo), z: 8, core: 2. Of those that a mesh axis runs over, the one named last changes fastest.
Arguments:
- projected: bfloat16 [3, 64, 524288], P(None, None, ('seq', 'chan')), may hold values from -6 to 6
- live_blocks: int32 [4096], P('seq'), may hold values 0 or 1
- filters: float32 [4, 524288], P('chan', 'seq'), as said below
- skip_gain: float32 [64], P('chan'), may hold values from -2 to 2
Outputs:
- gated: bfloat16 [64, 524288], P('chan', 'seq')
The draws below stay inside these ranges and needn't reach their ends.
Inputs may be any that keep to these rules, and one draw needn't show every extreme that they name: filters holds finite float32 taps.
All inputs are finite; a program needn't handle non-finite values. No bound on the sum of `live_blocks` on one device may be relied on, other than what follows from the above.
Results may differ from the reference program's by a relative error of at most 0.0049.
Values may be sent and summed in bfloat16 or wider, within the bound.
No kernel may reach another device: no remote copies, remote signals or barrier semaphores. Data moves between devices by JAX's collectives and lax.ppermute only.
A program may use at most 128 MiB of HBM per device.

```python
import math
import jax
import jax.numpy as jnp
from jax import lax

C = 64
GROUP = 16
R = 128
N = 1048576
L = 524288
G = 4


def draw_filters(key, part):
    key = jax.random.fold_in(key, 11)
    first_key, second_key = jax.random.split(key, 2)
    taps = jnp.arange(L, dtype=jnp.float32)
    order = jnp.arange(G, dtype=jnp.float32)
    spread = (order + jax.random.uniform(first_key, (G,), jnp.float32)) / G
    reach = L * jnp.exp(-math.log(16.0) * spread)
    slow_part = jnp.exp(-taps[None, :] / reach[:, None]) * jnp.sqrt(2.0 / reach)[:, None]
    fast_part = 0.5 * jnp.exp(-taps / 16.0)
    envelope = fast_part[None, :] + slow_part
    noise = jax.random.normal(second_key, (G, L), jnp.float32)
    return (noise * envelope).astype(jnp.float32)


def touch_ends(array, own_key, smallest, high):
    place = [jax.random.randint(jax.random.fold_in(own_key, axis), (), 0, length) for axis, length in enumerate(array.shape)]
    longest = array.shape.index(max(array.shape))
    beside = place[:longest] + [(place[longest] + 1) % array.shape[longest]] + place[longest + 1:]
    return array.at[tuple(place)].set(smallest).at[tuple(beside)].set(high)


def levels(key, shape, cuts, least, largest):
    def one(position, blocks):
        steps = jax.random.uniform(jax.random.fold_in(jax.random.fold_in(key, 6), position), (blocks,), jnp.float32, least / len(cuts), largest / len(cuts))
        return jnp.repeat(jnp.exp(steps), shape[position] // blocks).reshape((-1,) + (1,) * (len(shape) - position - 1))

    gain = one(*cuts[0])
    for cut in cuts[1:]:
        gain = gain * one(*cut)
    return gain


def scatter_about(rng, extent, deviation, most, cuts=(), kind=jnp.bfloat16):
    factor_of = levels(rng, extent, cuts, -0.22, 0.18) if cuts else 1.0
    values = jax.random.normal(rng, extent, jnp.float32) * deviation * factor_of
    return jnp.minimum(jnp.maximum(values, -most), most).astype(kind)


def setup_inputs(seed: int = 0) -> dict:
    streams_of = jax.random.split(jax.random.key(seed), 5)
    projected = scatter_about(streams_of[0], (3, C, L), 1.0, 6.0, ((2, 512),))
    live_blocks = touch_ends((jax.random.randint(streams_of[1], (L // R,), 0, 4) < 3).astype(jnp.int32), jax.random.fold_in(streams_of[1], 1), 0, 1)
    filters = draw_filters(jax.random.fold_in(streams_of[4], 71), 0)
    skip_gain = scatter_about(streams_of[3], (C,), 0.5, 2.0, ((0, 4),), jnp.float32)
    return {"projected": projected, "live_blocks": live_blocks, "filters": filters, "skip_gain": skip_gain}


def reference(projected, live_blocks, filters, skip_gain):
    gate_rows = projected[0].astype(jnp.float32)
    key_rows = projected[1].astype(jnp.float32)
    value_rows = projected[2].astype(jnp.float32)
    keep_mask = jnp.broadcast_to(live_blocks[:, None], (L // R, R)).reshape(L).astype(jnp.float32)
    product_rows = (key_rows * value_rows * keep_mask[None, :]).astype(jnp.bfloat16)

    def one_group(group_id):
        channel_rows = lax.dynamic_slice_in_dim(product_rows, group_id * GROUP, GROUP, 0).astype(jnp.float32)
        filter_row = lax.dynamic_slice_in_dim(filters, group_id, 1, 0)
        filter_spec = jnp.fft.rfft(filter_row, n=N, axis=-1)
        spectra = jnp.fft.rfft(channel_rows, n=N, axis=-1)
        filtered = spectra * filter_spec
        convolved = jnp.fft.irfft(filtered, n=N, axis=-1)[:, :L]
        return convolved.astype(jnp.float32)

    convolved = lax.map(one_group, jnp.arange(G, dtype=jnp.int32)).reshape(C, L)
    direct = skip_gain[:, None] * product_rows.astype(jnp.float32)
    return (gate_rows * (convolved + direct)).astype(jnp.bfloat16)
```

```python
from functools import partial

import jax
import jax.numpy as jnp
import ml_dtypes
import numpy as np
from jax import lax
from jax.experimental import pallas as pl
from jax.experimental.pallas import tpu as pltpu
from jax.sharding import PartitionSpec as P

BLOCK = 1024
SEQ = 128
CHAN = 4
GROUP = 16
FREQ = BLOCK // SEQ
LANES = 128
VMEM = 48 * 1024 * 1024


def wave_tables():
    k = np.arange(BLOCK, dtype=np.int64)[:, None]
    t = np.arange(BLOCK, dtype=np.int64)[None, :]
    angle = 2.0 * np.pi * ((2 * k + 1) * t % (4 * BLOCK)) / (4 * BLOCK)
    return np.stack([np.cos(angle), -np.sin(angle)]).astype(ml_dtypes.bfloat16)


def lane_ids(shape):
    return lax.broadcasted_iota(jnp.int32, shape, len(shape) - 1)


def row_ids(shape):
    return lax.broadcasted_iota(jnp.int32, shape, len(shape) - 2)


def swap_parts(v):
    is_real = (lane_ids(v.shape) // GROUP) % 2 == 0
    up = pltpu.roll(v, LANES - GROUP, 1)
    down = pltpu.roll(v, GROUP, 1)
    return jnp.where(is_real, -up, down)


def product_kernel(live_ref, proj_ref, out_ref):
    first = lax.axis_index("chan") * (BLOCK // 128)
    for part in range(BLOCK // 128):
        at = pl.ds(part * 128, 128)
        keep = live_ref[first + part].astype(jnp.float32)
        for j in range(CHAN):
            rows = pl.ds(j * GROUP, GROUP)
            key = proj_ref[1, rows, at].astype(jnp.float32)
            value = proj_ref[2, rows, at].astype(jnp.float32)
            out_ref[j, pl.ds(0, GROUP), at] = proj_ref[0, rows, at]
            out_ref[j, pl.ds(GROUP, GROUP), at] = (key * value * keep).astype(jnp.bfloat16)


def masked_product(live_blocks, projected):
    return pl.pallas_call(
        product_kernel,
        out_shape=jax.ShapeDtypeStruct((CHAN, 2 * GROUP, BLOCK), jnp.bfloat16),
        in_specs=[
            pl.BlockSpec(memory_space=pltpu.SMEM),
            pl.BlockSpec(memory_space=pltpu.VMEM),
        ],
        out_specs=pl.BlockSpec(memory_space=pltpu.VMEM),
        compiler_params=pltpu.CompilerParams(vmem_limit_bytes=VMEM),
        name="masked_product",
    )(live_blocks, projected)


FWD_TILE = 256


def forward_kernel(rows_ref, taps_ref, wave_ref, out_ref, cols):
    @pl.when(pl.program_id(0) == 0)
    def _():
        for j in range(CHAN):
            part = rows_ref[j, pl.ds(GROUP, GROUP), :].astype(jnp.float32)
            both = jnp.concatenate([part, part], axis=0)
            cols[:, pl.ds(j * 2 * GROUP, 2 * GROUP)] = both.T.astype(jnp.bfloat16)
        taps = taps_ref[...]
        high = taps.astype(jnp.bfloat16).astype(jnp.float32)
        low = taps - high
        stacked = [v[j : j + 1, :] for v in (high, low) for j in range(CHAN) for _ in (0, 1)]
        stacked.append(jnp.zeros((LANES - 4 * CHAN, BLOCK), jnp.float32))
        cols[:, pl.ds(LANES, LANES)] = jnp.concatenate(stacked, axis=0).T.astype(jnp.bfloat16)

    weights = cols[...]
    real = jnp.dot(wave_ref[0], weights, preferred_element_type=jnp.float32)
    imag = jnp.dot(wave_ref[1], weights, preferred_element_type=jnp.float32)
    lane = lane_ids((FWD_TILE, LANES))
    signal = jnp.where((lane // GROUP) % 2 == 0, real[:, :LANES], imag[:, :LANES])
    taps = jnp.where(lane % 2 == 0, real[:, LANES:], imag[:, LANES:])
    taps = taps + pltpu.roll(taps, LANES - 2 * CHAN, 1)
    high = taps.astype(jnp.bfloat16).astype(jnp.float32)
    low = pltpu.roll(taps - high, 2 * CHAN, 1)
    taps = jnp.where(lane < 2 * CHAN, high, jnp.where(lane < 4 * CHAN, low, 0.0))
    shape = (FWD_TILE // FREQ, FREQ, LANES)
    both = jnp.concatenate([signal.reshape(shape), taps.reshape(shape)], axis=1)
    out_ref[...] = both.astype(jnp.bfloat16)


def forward_blocks(rows, taps, wave):
    steps = BLOCK // FWD_TILE
    return pl.pallas_call(
        forward_kernel,
        grid=(steps,),
        out_shape=jax.ShapeDtypeStruct((SEQ, 2 * FREQ, LANES), jnp.bfloat16),
        in_specs=[
            pl.BlockSpec((CHAN, 2 * GROUP, BLOCK), lambda i: (0, 0, 0)),
            pl.BlockSpec((CHAN, BLOCK), lambda i: (0, 0)),
            pl.BlockSpec((2, FWD_TILE, BLOCK), lambda i: (0, i, 0)),
        ],
        out_specs=pl.BlockSpec((FWD_TILE // FREQ, 2 * FREQ, LANES), lambda i: (i, 0, 0)),
        scratch_shapes=[pltpu.VMEM((BLOCK, 2 * LANES), jnp.bfloat16)],
        compiler_params=pltpu.CompilerParams(vmem_limit_bytes=VMEM),
        name="forward_blocks",
    )(rows, taps, wave)


def mix_kernel(in_ref, out_ref, spread, wide, matrix):
    spread[...] = in_ref[...].astype(jnp.float32)
    square = (SEQ, LANES)
    row, lane = row_ids(square), lane_ids(square)
    comb = spread[:, FREQ, :]
    for k in range(1, FREQ):
        comb = comb + pltpu.roll(spread[:, FREQ + k, :], k * 4 * CHAN, 1)
    negate = jnp.where((row + lane) % SEQ == 0, 1.0, 0.0).astype(jnp.bfloat16)
    turned = jnp.dot(comb.T.astype(jnp.bfloat16), negate, preferred_element_type=jnp.float32)
    causal = lane <= row
    small = (2 * CHAN, SEQ)
    small_row, small_lane = row_ids(small), lane_ids(small)
    for k in range(FREQ):
        base = k * 4 * CHAN
        spec = turned[base : base + 2 * CHAN, :] + turned[base + 2 * CHAN : base + 4 * CHAN, :]
        late = jnp.where(small_lane == 0, 0.0, pltpu.roll(spec, SEQ - 1, 1))
        before = jnp.where(small_row >= 2 * CHAN - 2, late, spec)
        sign = -1.0 if k % 2 else 1.0
        spec = spec + sign * jnp.where(
            small_row % 2 == 0, -pltpu.roll(before, 1, 0), pltpu.roll(before, 3, 0)
        )
        for q in range(CHAN):
            for part in range(2):
                line = spec[2 * q + part : 2 * q + part + 1, :]
                tall = jnp.broadcast_to(line, square)
                toeplitz = pltpu.roll(tall, 0, 1, stride=1, stride_axis=0)
                toeplitz = jnp.where(causal, toeplitz, 0.0)
                matrix[pl.ds(part * SEQ, SEQ), pl.ds(q * SEQ, SEQ)] = toeplitz.astype(jnp.bfloat16)
        signal = spread[:, k, :]
        late = jnp.where(row == 0, 0.0, pltpu.roll(signal, 1, 0))
        shifted = [signal.astype(jnp.bfloat16)]
        for q in range(1, CHAN):
            move = 2 * GROUP * q
            moved = jnp.where(lane >= LANES - move, late, signal)
            shifted.append(pltpu.roll(moved, move, 1).astype(jnp.bfloat16))
        parts = jnp.dot(
            matrix[...], jnp.concatenate(shifted, axis=0), preferred_element_type=jnp.float32
        )
        wide[:, k, :] = parts[:SEQ, :] + swap_parts(parts[SEQ:, :])
    out_ref[...] = wide[...].astype(jnp.bfloat16)


def mix_blocks(received):
    return pl.pallas_call(
        mix_kernel,
        out_shape=jax.ShapeDtypeStruct((SEQ, FREQ, LANES), jnp.bfloat16),
        in_specs=[pl.BlockSpec(memory_space=pltpu.VMEM)],
        out_specs=pl.BlockSpec(memory_space=pltpu.VMEM),
        scratch_shapes=[
            pltpu.VMEM((SEQ, 2 * FREQ, LANES), jnp.float32),
            pltpu.VMEM((SEQ, FREQ, LANES), jnp.float32),
            pltpu.VMEM((2 * SEQ, CHAN * SEQ), jnp.bfloat16),
        ],
        compiler_params=pltpu.CompilerParams(vmem_limit_bytes=VMEM),
        name="mix_blocks",
    )(received)


INV_TILE = 256


def inverse_kernel(spec_ref, rows_ref, gain_ref, wave_ref, out_ref, turned):
    step = pl.program_id(0)

    @pl.when(step == 0)
    def _():
        turned[...] = spec_ref[...].astype(jnp.float32).T.astype(jnp.bfloat16)

    spec = turned[...]
    real = jnp.dot(spec, wave_ref[0], preferred_element_type=jnp.float32)
    imag = jnp.dot(spec, wave_ref[1], preferred_element_type=jnp.float32)
    gain = gain_ref[...]
    for p in range(CHAN):
        base = 2 * GROUP * p
        value = real[base : base + GROUP, :] + imag[base + GROUP : base + 2 * GROUP, :]
        value = value * (1.0 / BLOCK)
        gate = rows_ref[p, pl.ds(0, GROUP), :].astype(jnp.float32)
        direct = rows_ref[p, pl.ds(GROUP, GROUP), :].astype(jnp.float32)
        at = pl.ds(pl.multiple_of(p * BLOCK + step * INV_TILE, INV_TILE), INV_TILE)
        out_ref[:, at] = (gate * (value + gain * direct)).astype(jnp.bfloat16)


def inverse_blocks(spec, rows, gain, wave):
    steps = BLOCK // INV_TILE
    return pl.pallas_call(
        inverse_kernel,
        grid=(steps,),
        out_shape=jax.ShapeDtypeStruct((GROUP, CHAN * BLOCK), jnp.bfloat16),
        in_specs=[
            pl.BlockSpec((BLOCK, LANES), lambda i: (0, 0)),
            pl.BlockSpec((CHAN, 2 * GROUP, INV_TILE), lambda i: (0, 0, i)),
            pl.BlockSpec((GROUP, 1), lambda i: (0, 0)),
            pl.BlockSpec((2, BLOCK, INV_TILE), lambda i: (0, 0, i)),
        ],
        out_specs=pl.BlockSpec((GROUP, CHAN * BLOCK), lambda i: (0, 0)),
        scratch_shapes=[pltpu.VMEM((LANES, BLOCK), jnp.bfloat16)],
        compiler_params=pltpu.CompilerParams(vmem_limit_bytes=VMEM),
        name="inverse_blocks",
    )(spec, rows, gain, wave)


def body(projected, live_blocks, filters, skip_gain):
    exchange = partial(lax.all_to_all, split_axis=0, concat_axis=0, tiled=True)
    wave = jnp.asarray(wave_tables())
    rows = exchange(masked_product(live_blocks, projected), "chan")
    sent = forward_blocks(rows, filters.reshape(CHAN, BLOCK), wave)
    mixed = mix_blocks(exchange(sent, "seq"))
    spec = exchange(mixed, "seq").reshape(BLOCK, LANES)
    return inverse_blocks(spec, rows, skip_gain.reshape(GROUP, 1), wave)


def solution(mesh):
    in_specs = (P(None, None, ("seq", "chan")), P("seq"), P("chan", "seq"), P("chan"))
    out_specs = P("chan", "seq")
    return jax.shard_map(body, mesh=mesh, in_specs=in_specs, out_specs=out_specs, check_vma=False)
```

```python
from functools import partial

import jax
import jax.numpy as jnp
import ml_dtypes
import numpy as np
from jax import lax
from jax.experimental import pallas as pl
from jax.experimental.pallas import tpu as pltpu
from jax.sharding import Mesh, PartitionSpec as P

BLOCK = 1024
SEQ = 128
CHAN = 4
GROUP = 16
FREQ = BLOCK // SEQ
LANES = 128
HALF = 64
SIGNAL = 4
MESSAGE = 6
PAIR = 2 * MESSAGE
MIB = 1024 * 1024
COST = pl.CostEstimate(flops=6_000_000_000, bytes_accessed=20_000_000, transcendentals=0)
ON_CHIP = pl.BlockSpec(memory_space=pltpu.VMEM)


BASE = BLOCK // 2
QUAD = FREQ // 2


def wave_tables():
    k = np.arange(BASE, dtype=np.int64).reshape(SEQ, QUAD).T.reshape(BASE, 1)
    t = np.arange(BLOCK, dtype=np.int64)[None, :]
    angle = 2.0 * np.pi * ((2 * k + 1) * t % (4 * BLOCK)) / (4 * BLOCK)
    return np.stack([np.cos(angle), -np.sin(angle)]).astype(ml_dtypes.bfloat16)


def lane_ids(shape):
    return lax.broadcasted_iota(jnp.int32, shape, len(shape) - 1)


def row_ids(shape):
    return lax.broadcasted_iota(jnp.int32, shape, len(shape) - 2)


def swap_parts(v):
    is_real = (lane_ids(v.shape) // GROUP) % 2 == 0
    up = pltpu.roll(v, LANES - GROUP, 1)
    down = pltpu.roll(v, GROUP, 1)
    return jnp.where(is_real, -up, down)


def gain_kernel(gain_ref, out_ref):
    out_ref[...] = jnp.concatenate([gain_ref[...]] * (LANES // GROUP), axis=1)


def lane_gains(skip_gain):
    return pl.pallas_call(
        gain_kernel,
        out_shape=jax.ShapeDtypeStruct((1, LANES), jnp.float32),
        in_specs=[ON_CHIP],
        out_specs=ON_CHIP,
        compiler_params=pltpu.CompilerParams(vmem_limit_bytes=60 * MIB),
        cost_estimate=COST,
        name="lane_gains",
    )(skip_gain.reshape(1, GROUP))


def forward_kernel(
    live_ref, own_ref, got_ref, taps_ref, wave, out_ref, gate_ref, send_ref, cols, packed
):
    high, core = lax.axis_index("yh"), lax.axis_index("core")
    count = 4 * GROUP
    piece = (GROUP, LANES)
    even = lane_ids(piece) % 2 == 0
    for part in range(2):
        rows = pl.ds(pl.multiple_of((2 * part + core) * GROUP, GROUP), GROUP)
        for blk in range(2):

            def read(i, at):
                return jnp.where(core == blk, own_ref[i, rows, at], got_ref[i, rows, at])

            to = (2 * part + blk) * GROUP
            for block in range(BLOCK // LANES):
                at = pl.ds(block * LANES, LANES)
                live = live_ref[(2 * high + blk) * (BLOCK // LANES) + block].astype(jnp.float32)
                key, value = read(1, at).astype(jnp.float32), read(2, at).astype(jnp.float32)
                value = key * value * live
                cols[pl.ds(to, GROUP), at] = jnp.where(even, value, 0.0).astype(jnp.bfloat16)
                cols[pl.ds(count + to, GROUP), at] = jnp.where(even, 0.0, value).astype(
                    jnp.bfloat16
                )
            gate = read(0, slice(None))

            @pl.when(high == part)
            def _():
                gate_ref[blk] = gate

            @pl.when(high != part)
            def _():
                send_ref[blk] = gate

    even = lane_ids((GROUP, BLOCK)) % 2 == 0
    taps = jnp.concatenate(
        [taps_ref[:, j * BLOCK : (j + 1) * BLOCK] for j in range(CHAN)], axis=0
    )
    top = taps.astype(jnp.bfloat16).astype(jnp.float32)
    taps = jnp.concatenate([top, taps - top, top, taps - top], axis=0)
    kept = even == (row_ids((GROUP, BLOCK)) < 2 * CHAN)
    cols[pl.ds(LANES, GROUP), :] = jnp.where(kept, taps, 0.0).astype(jnp.bfloat16)
    cols[pl.ds(LANES + GROUP, LANES - GROUP), :] = jnp.zeros(
        (LANES - GROUP, BLOCK), jnp.bfloat16
    )
    weights = cols[...]
    sums = []
    for i in range(2):
        sums.append(
            lax.dot_general(
                wave[i], weights, (((1,), (1,)), ((), ())), preferred_element_type=jnp.float32
            )
        )

    def put(row, value):
        packed[pl.ds(row, SEQ, stride=PAIR), :] = value

    square = (SEQ, LANES)
    lane = lane_ids(square)
    comb = jnp.zeros(square, jnp.float32)
    for i in range(QUAD):
        at = slice(i * SEQ, (i + 1) * SEQ)
        cos, sin = sums[0][at, :LANES], sums[1][at, :LANES]
        turn_cos, turn_sin = pltpu.roll(cos, HALF, 1), pltpu.roll(sin, HALF, 1)
        real = jnp.where(lane < HALF, cos + turn_cos, turn_cos - cos)
        imag = jnp.where(lane < HALF, sin + turn_sin, sin - turn_sin)
        place = (lane % HALF) // GROUP
        middle = pltpu.roll(jnp.where(place == 0, imag, real), GROUP, 1)
        last = pltpu.roll(imag, 2 * GROUP, 1)
        put(i, jnp.where(place == 0, real, jnp.where(place == 3, last, middle)))
        middle = pltpu.roll(jnp.where(place == 2, imag, real), LANES - GROUP, 1)
        last = pltpu.roll(real, LANES - 2 * GROUP, 1)
        put(MESSAGE + i, jnp.where(place == 3, imag, jnp.where(place == 0, last, middle)))
        for part in range(2):
            move = part * HALF + i * GROUP
            value = sums[part][at, LANES:]
            comb = comb + (pltpu.roll(value, move, 1) if move else value)
    step = 2 * CHAN
    difference = pltpu.roll(comb, step, 1) - comb
    difference = jnp.where(lane < HALF, difference, -difference)
    both = comb + pltpu.roll(comb, LANES - step, 1)
    comb = jnp.where((lane // step) % 2 == 0, both, difference)
    comb = comb + pltpu.roll(comb, LANES - CHAN, 1)
    top = comb.astype(jnp.bfloat16).astype(jnp.float32)
    comb = jnp.where((lane // CHAN) % 2 == 0, top, pltpu.roll(comb - top, CHAN, 1))
    put(SIGNAL, jnp.where(high == 0, comb, 0.0))
    put(MESSAGE + SIGNAL, jnp.where(high == 1, comb, 0.0))
    empty = jnp.zeros(square, jnp.float32)
    put(SIGNAL + 1, empty)
    put(MESSAGE + SIGNAL + 1, empty)
    out_ref[...] = packed[...].astype(jnp.bfloat16)


def forward_blocks(live_blocks, own, got, taps, wave):
    gate = jax.ShapeDtypeStruct((2, GROUP, BLOCK), jnp.bfloat16)
    return pl.pallas_call(
        forward_kernel,
        out_shape=[jax.ShapeDtypeStruct((SEQ * PAIR, LANES), jnp.bfloat16), gate, gate],
        in_specs=[pl.BlockSpec(memory_space=pltpu.SMEM)] + [ON_CHIP] * 4,
        out_specs=[ON_CHIP] * 3,
        scratch_shapes=[
            pltpu.VMEM((2 * LANES, BLOCK), jnp.bfloat16),
            pltpu.VMEM((SEQ * PAIR, LANES), jnp.float32),
        ],
        compiler_params=pltpu.CompilerParams(vmem_limit_bytes=48 * MIB),
        name="forward_blocks",
    )(live_blocks, own, got, taps, wave)


def mix_kernel(in_ref, gain_ref, out_ref, spread, wide, matrix):
    spread[...] = in_ref[...].astype(jnp.float32)
    square = (SEQ, LANES)
    row, lane = row_ids(square), lane_ids(square)

    def take(at):
        return spread[pl.ds(at, SEQ, stride=PAIR), :]

    comb = take(SIGNAL) + take(MESSAGE + SIGNAL)
    negate = jnp.where((row + lane) % SEQ == 0, 1.0, 0.0).astype(jnp.bfloat16)
    turned = jnp.dot(comb.T.astype(jnp.bfloat16), negate, preferred_element_type=jnp.float32)
    turned = turned + pltpu.roll(turned, LANES - CHAN, 0)
    late = jnp.where(lane == 0, 0.0, pltpu.roll(turned, SEQ - 1, 1))
    before = jnp.where(
        row % CHAN == 0, pltpu.roll(late, LANES - CHAN + 1, 0), pltpu.roll(turned, 1, 0)
    )
    half_row = row_ids((HALF, LANES))
    flip = (half_row // (4 * CHAN) + half_row // (2 * CHAN)) % 2 == 1
    before = jnp.where(jnp.concatenate([flip, flip], axis=0), -before, before)
    spec = (turned[:HALF] - before[HALF:], turned[HALF:] + before[:HALF])
    causal = lane <= row
    gain = gain_ref[...]
    is_real = (lane // GROUP) % 2 == 0
    for k in range(FREQ):
        digit, mirror = k // 2, k % 2
        base = digit * 4 * CHAN + mirror * 2 * CHAN
        for q in range(CHAN):
            for part in range(2):
                line = spec[part][base + q : base + q + 1, :]
                tall = jnp.broadcast_to(line, square)
                toeplitz = pltpu.roll(tall, 0, 1, stride=1, stride_axis=0)
                toeplitz = jnp.where(causal, toeplitz, 0.0)
                matrix[pl.ds(part * SEQ, SEQ), pl.ds(q * SEQ, SEQ)] = toeplitz.astype(jnp.bfloat16)
        low, high = take(digit), take(MESSAGE + digit)
        if mirror == 0:
            signal = jnp.where(lane < HALF, low, pltpu.roll(high, HALF, 1))
        else:
            signal = jnp.where(lane < HALF, pltpu.roll(low, HALF, 1), high)
        late = jnp.where(row == 0, 0.0, pltpu.roll(signal, 1, 0))
        shifted = [signal.astype(jnp.bfloat16)]
        for q in range(1, CHAN):
            move = 2 * GROUP * q
            moved = jnp.where(lane >= LANES - move, late, signal)
            shifted.append(pltpu.roll(moved, move, 1).astype(jnp.bfloat16))
        parts = jnp.dot(
            matrix[...], jnp.concatenate(shifted, axis=0), preferred_element_type=jnp.float32
        )
        mixed = parts[:SEQ, :] + swap_parts(parts[SEQ:, :]) + gain * signal
        if mirror == 0:
            first = mixed
            continue
        plus, minus = first + mixed, first - mixed
        wide[:, digit, :] = jnp.where(is_real, plus, minus)
        wide[:, QUAD + digit, :] = jnp.where(is_real, minus, plus)
    out_ref[...] = wide[...].astype(jnp.bfloat16)


def mix_blocks(received, gain):
    return pl.pallas_call(
        mix_kernel,
        out_shape=jax.ShapeDtypeStruct((SEQ, FREQ, LANES), jnp.bfloat16),
        in_specs=[ON_CHIP, ON_CHIP],
        out_specs=ON_CHIP,
        scratch_shapes=[
            pltpu.VMEM((SEQ * PAIR, LANES), jnp.float32),
            pltpu.VMEM((SEQ, FREQ, LANES), jnp.float32),
            pltpu.VMEM((2 * SEQ, CHAN * SEQ), jnp.bfloat16),
        ],
        compiler_params=pltpu.CompilerParams(vmem_limit_bytes=48 * MIB),
        cost_estimate=COST,
        name="mix_blocks",
    )(received, gain)


def inverse_kernel(spec_ref, gate_ref, other_ref, wave, out_ref, plain):
    plain[...] = spec_ref[...].astype(jnp.float32)
    sides = [
        [plain[pl.ds(part * QUAD + i, SEQ, stride=FREQ), :].T for i in range(QUAD)]
        for part in range(2)
    ]
    sides = [jnp.concatenate(side, axis=1).astype(jnp.bfloat16) for side in sides]
    total = None
    for part in range(2):
        lines = [
            side[(2 * p + part) * GROUP : (2 * p + part + 1) * GROUP, :]
            for side in sides
            for p in range(CHAN)
        ]
        term = jnp.dot(
            jnp.concatenate(lines, axis=0), wave[part], preferred_element_type=jnp.float32
        )
        total = term if total is None else total + term
    high = lax.axis_index("yh")
    even = lane_ids((GROUP, BLOCK)) % 2 == 0
    for p in range(CHAN):
        at = p * GROUP
        value = jnp.where(
            even, total[at : at + GROUP, :], total[HALF + at : HALF + at + GROUP, :]
        )
        gate = jnp.where(high == p // 2, gate_ref[p % 2], other_ref[p % 2]).astype(jnp.float32)
        out_ref[:, pl.ds(p * BLOCK, BLOCK)] = (gate * (value * (1.0 / BLOCK))).astype(jnp.bfloat16)


def inverse_blocks(spec, gate, other, wave):
    return pl.pallas_call(
        inverse_kernel,
        out_shape=jax.ShapeDtypeStruct((GROUP, CHAN * BLOCK), jnp.bfloat16),
        in_specs=[ON_CHIP] * 4,
        out_specs=ON_CHIP,
        scratch_shapes=[pltpu.VMEM((BLOCK, LANES), jnp.float32)],
        compiler_params=pltpu.CompilerParams(vmem_limit_bytes=48 * MIB),
        name="inverse_blocks",
    )(spec, gate, other, wave)


def body(projected, live_blocks, filters, skip_gain):
    exchange = partial(lax.all_to_all, split_axis=0, concat_axis=0, tiled=True)
    wave = jnp.asarray(wave_tables())
    swap = ((0, 1), (1, 0))
    got = lax.ppermute(projected, "core", swap)
    got, gain = lax.optimization_barrier((got, lane_gains(skip_gain)))
    sent, gate, send = forward_blocks(live_blocks, projected, got, filters, wave)
    other = lax.ppermute(send, "yh", swap)
    got_spec = exchange(sent.reshape(-1, 2, LANES), ("seq", "yh")).reshape(-1, LANES)
    mixed = mix_blocks(got_spec, gain)
    spec = exchange(mixed, "seq").reshape(BLOCK, LANES)
    return inverse_blocks(spec, gate, other, wave)


def solution(mesh):
    split = Mesh(mesh.devices.reshape(SEQ, 2, 2), ("seq", "yh", "core"))
    chan = ("yh", "core")
    in_specs = (P(None, None, ("seq", "yh", "core")), P("seq"), P(chan, "seq"), P(chan))
    out_specs = P(chan, "seq")
    return jax.shard_map(body, mesh=split, in_specs=in_specs, out_specs=out_specs, check_vma=False)
```

```python
from functools import partial

import jax
import jax.numpy as jnp
import ml_dtypes
import numpy as np
from jax import lax
from jax.experimental import pallas as pl
from jax.experimental.pallas import tpu as pltpu
from jax.sharding import Mesh, PartitionSpec as P

BLOCK = 1024
SEQ = 128
CHAN = 4
GROUP = 16
FREQ = BLOCK // SEQ
LANES = 128
HALF = 64
SIGNAL = 4
MESSAGE = 6
PAIR = 2 * MESSAGE
MIB = 1024 * 1024
COST = pl.CostEstimate(flops=6_000_000_000, bytes_accessed=20_000_000, transcendentals=0)
ON_CHIP = pl.BlockSpec(memory_space=pltpu.VMEM)


BASE = BLOCK // 2
QUAD = FREQ // 2


def wave_tables():
    k = np.arange(BASE, dtype=np.int64).reshape(SEQ, QUAD).T.reshape(BASE, 1)
    t = np.arange(BLOCK, dtype=np.int64)[None, :]
    angle = 2.0 * np.pi * ((2 * k + 1) * t % (4 * BLOCK)) / (4 * BLOCK)
    return np.stack([np.cos(angle), -np.sin(angle)]).astype(ml_dtypes.bfloat16)


def lane_ids(shape):
    return lax.broadcasted_iota(jnp.int32, shape, len(shape) - 1)


def row_ids(shape):
    return lax.broadcasted_iota(jnp.int32, shape, len(shape) - 2)


def swap_parts(v):
    turned = pltpu.roll(v, HALF, 1)
    return jnp.where(lane_ids(v.shape) < HALF, -turned, turned)


def gain_kernel(gain_ref, out_ref):
    out_ref[...] = jnp.concatenate([gain_ref[...]] * (LANES // GROUP), axis=1)


def lane_gains(skip_gain):
    return pl.pallas_call(
        gain_kernel,
        out_shape=jax.ShapeDtypeStruct((1, LANES), jnp.float32),
        in_specs=[ON_CHIP],
        out_specs=ON_CHIP,
        compiler_params=pltpu.CompilerParams(vmem_limit_bytes=60 * MIB),
        cost_estimate=COST,
        name="lane_gains",
    )(skip_gain.reshape(1, GROUP))


def forward_kernel(
    live_ref, own_ref, got_ref, taps_ref, wave, out_ref, gate_ref, send_ref, cols, packed
):
    high, core = lax.axis_index("yh"), lax.axis_index("core")
    side = 2 * GROUP
    piece = (GROUP, LANES)
    even = lane_ids(piece) % 2 == 0
    for part in range(2):
        rows = pl.ds(pl.multiple_of((2 * part + core) * GROUP, GROUP), GROUP)
        for blk in range(2):

            def read(i, at):
                return jnp.where(core == blk, own_ref[i, rows, at], got_ref[i, rows, at])

            to = part * HALF + blk * GROUP
            for block in range(BLOCK // LANES):
                at = pl.ds(block * LANES, LANES)
                live = live_ref[(2 * high + blk) * (BLOCK // LANES) + block].astype(jnp.float32)
                key, value = read(1, at).astype(jnp.float32), read(2, at).astype(jnp.float32)
                value = key * value * live
                cols[pl.ds(to, GROUP), at] = value.astype(jnp.bfloat16)
                value = jnp.where(even, value, -value)
                cols[pl.ds(to + side, GROUP), at] = value.astype(jnp.bfloat16)
            gate = read(0, slice(None))

            @pl.when(high == part)
            def _():
                gate_ref[blk] = gate

            @pl.when(high != part)
            def _():
                send_ref[blk] = gate

    even = lane_ids((GROUP, BLOCK)) % 2 == 0
    taps = jnp.concatenate(
        [taps_ref[:, j * BLOCK : (j + 1) * BLOCK] for j in range(CHAN)], axis=0
    )
    top = taps.astype(jnp.bfloat16).astype(jnp.float32)
    taps = jnp.concatenate([top, taps - top, top, taps - top], axis=0)
    plain = even | (row_ids((GROUP, BLOCK)) < 2 * CHAN)
    cols[pl.ds(LANES, GROUP), :] = jnp.where(plain, taps, -taps).astype(jnp.bfloat16)
    cols[pl.ds(LANES + GROUP, LANES - GROUP), :] = jnp.zeros(
        (LANES - GROUP, BLOCK), jnp.bfloat16
    )
    weights = cols[...]
    sums = []
    for i in range(2):
        sums.append(
            lax.dot_general(
                wave[i], weights, (((1,), (1,)), ((), ())), preferred_element_type=jnp.float32
            )
        )

    def put(row, value):
        packed[pl.ds(row, SEQ, stride=PAIR), :] = value

    square = (SEQ, LANES)
    lane = lane_ids(square)
    comb = jnp.zeros(square, jnp.float32)
    for i in range(QUAD):
        at = slice(i * SEQ, (i + 1) * SEQ)
        cos, sin = sums[0][at, :LANES], sums[1][at, :LANES]
        sin = jnp.where(lane % HALF < side, sin, -sin)
        put(i, jnp.where(lane < HALF, cos, pltpu.roll(sin, HALF, 1)))
        put(MESSAGE + i, jnp.where(lane < HALF, pltpu.roll(cos, HALF, 1), sin))
        for part in range(2):
            move = part * HALF + i * GROUP
            value = sums[part][at, LANES:]
            comb = comb + (pltpu.roll(value, move, 1) if move else value)
    comb = jnp.where((lane >= HALF) & ((lane // (2 * CHAN)) % 2 == 1), -comb, comb)
    comb = comb + pltpu.roll(comb, LANES - CHAN, 1)
    top = comb.astype(jnp.bfloat16).astype(jnp.float32)
    comb = jnp.where((lane // CHAN) % 2 == 0, top, pltpu.roll(comb - top, CHAN, 1))
    put(SIGNAL, jnp.where(high == 0, comb, 0.0))
    put(MESSAGE + SIGNAL, jnp.where(high == 1, comb, 0.0))
    empty = jnp.zeros(square, jnp.float32)
    put(SIGNAL + 1, empty)
    put(MESSAGE + SIGNAL + 1, empty)
    out_ref[...] = packed[...].astype(jnp.bfloat16)


def forward_blocks(live_blocks, own, got, taps, wave):
    gate = jax.ShapeDtypeStruct((2, GROUP, BLOCK), jnp.bfloat16)
    return pl.pallas_call(
        forward_kernel,
        out_shape=[jax.ShapeDtypeStruct((SEQ * PAIR, LANES), jnp.bfloat16), gate, gate],
        in_specs=[pl.BlockSpec(memory_space=pltpu.SMEM)] + [ON_CHIP] * 4,
        out_specs=[ON_CHIP] * 3,
        scratch_shapes=[
            pltpu.VMEM((2 * LANES, BLOCK), jnp.bfloat16),
            pltpu.VMEM((SEQ * PAIR, LANES), jnp.float32),
        ],
        compiler_params=pltpu.CompilerParams(vmem_limit_bytes=48 * MIB),
        name="forward_blocks",
    )(live_blocks, own, got, taps, wave)


def mix_kernel(in_ref, gain_ref, out_ref, spread, wide, matrix):
    spread[...] = in_ref[...].astype(jnp.float32)
    square = (SEQ, LANES)
    row, lane = row_ids(square), lane_ids(square)

    def take(at):
        return spread[pl.ds(at, SEQ, stride=PAIR), :]

    comb = take(SIGNAL) + take(MESSAGE + SIGNAL)
    negate = jnp.where((row + lane) % SEQ == 0, 1.0, 0.0).astype(jnp.bfloat16)
    turned = jnp.dot(comb.T.astype(jnp.bfloat16), negate, preferred_element_type=jnp.float32)
    turned = turned + pltpu.roll(turned, LANES - CHAN, 0)
    late = jnp.where(lane == 0, 0.0, pltpu.roll(turned, SEQ - 1, 1))
    before = jnp.where(
        row % CHAN == 0, pltpu.roll(late, LANES - CHAN + 1, 0), pltpu.roll(turned, 1, 0)
    )
    half_row = row_ids((HALF, LANES))
    flip = (half_row // (4 * CHAN) + half_row // (2 * CHAN)) % 2 == 1
    before = jnp.where(jnp.concatenate([flip, flip], axis=0), -before, before)
    spec = (turned[:HALF] - before[HALF:], turned[HALF:] + before[:HALF])
    causal = lane <= row
    gain = gain_ref[...]
    low_lane = lane % HALF < 2 * GROUP
    signals, rows = [], []
    for k in range(FREQ):
        digit, mirror = k // 2, k % 2
        low, high = take(digit), take(MESSAGE + digit)
        if mirror == 0:
            signal = jnp.where(low_lane, low, pltpu.roll(high, 2 * GROUP, 1))
        else:
            signal = jnp.where(low_lane, pltpu.roll(low, LANES - 2 * GROUP, 1), high)
        late = jnp.where(row == 0, 0.0, pltpu.roll(signal, 1, 0))
        signals.append(signal)
        rows.append(jnp.concatenate([signal, late], axis=1).astype(jnp.bfloat16))
    rows = jnp.concatenate(rows, axis=0)
    shape = (2 * LANES, (CHAN - 1) * LANES)
    source, target = row_ids(shape), lane_ids(shape)
    place = source % HALF + GROUP * (target // LANES + 1) - jnp.where(source < LANES, 0, HALF)
    same_part = (source // HALF) % 2 == (target // HALF) % 2
    shifts = jnp.where(same_part & (place == target % HALF), 1.0, 0.0).astype(jnp.bfloat16)
    moved = jnp.dot(rows, shifts, preferred_element_type=jnp.float32).astype(jnp.bfloat16)
    for k in range(FREQ):
        digit, mirror = k // 2, k % 2
        base = digit * 4 * CHAN + mirror * 2 * CHAN
        for q in range(CHAN):
            for part in range(2):
                line = spec[part][base + q : base + q + 1, :]
                tall = jnp.broadcast_to(line, square)
                toeplitz = pltpu.roll(tall, 0, 1, stride=1, stride_axis=0)
                toeplitz = jnp.where(causal, toeplitz, 0.0)
                matrix[pl.ds(part * SEQ, SEQ), pl.ds(q * SEQ, SEQ)] = toeplitz.astype(jnp.bfloat16)
        signal = signals[k]
        at = slice(k * SEQ, (k + 1) * SEQ)
        shifted = [rows[at, :LANES]]
        shifted += [moved[at, q * LANES : (q + 1) * LANES] for q in range(CHAN - 1)]
        parts = jnp.dot(
            matrix[...], jnp.concatenate(shifted, axis=0), preferred_element_type=jnp.float32
        )
        mixed = parts[:SEQ, :] + swap_parts(parts[SEQ:, :]) + gain * signal
        if mirror == 0:
            first = mixed
            continue
        plus, minus = first + mixed, first - mixed
        wide[:, digit, :] = jnp.where(lane < HALF, plus, minus)
        wide[:, QUAD + digit, :] = jnp.where(lane < HALF, minus, plus)
    out_ref[...] = wide[...].astype(jnp.bfloat16)


def mix_blocks(received, gain):
    return pl.pallas_call(
        mix_kernel,
        out_shape=jax.ShapeDtypeStruct((SEQ, FREQ, LANES), jnp.bfloat16),
        in_specs=[ON_CHIP, ON_CHIP],
        out_specs=ON_CHIP,
        scratch_shapes=[
            pltpu.VMEM((SEQ * PAIR, LANES), jnp.float32),
            pltpu.VMEM((SEQ, FREQ, LANES), jnp.float32),
            pltpu.VMEM((2 * SEQ, CHAN * SEQ), jnp.bfloat16),
        ],
        compiler_params=pltpu.CompilerParams(vmem_limit_bytes=48 * MIB),
        cost_estimate=COST,
        name="mix_blocks",
    )(received, gain)


def inverse_kernel(spec_ref, gate_ref, other_ref, wave, out_ref, plain):
    plain[...] = spec_ref[...].astype(jnp.float32)
    sides = [
        [plain[pl.ds(part * QUAD + i, SEQ, stride=FREQ), :].T for i in range(QUAD)]
        for part in range(2)
    ]
    sides = [jnp.concatenate(side, axis=1).astype(jnp.bfloat16) for side in sides]
    total = None
    for part in range(2):
        lines = [side[part * HALF : (part + 1) * HALF, :] for side in sides]
        term = jnp.dot(
            jnp.concatenate(lines, axis=0), wave[part], preferred_element_type=jnp.float32
        )
        total = term if total is None else total + term
    high = lax.axis_index("yh")
    even = lane_ids((GROUP, BLOCK)) % 2 == 0
    for p in range(CHAN):
        at = p * GROUP
        value = jnp.where(
            even, total[at : at + GROUP, :], total[HALF + at : HALF + at + GROUP, :]
        )
        gate = jnp.where(high == p // 2, gate_ref[p % 2], other_ref[p % 2]).astype(jnp.float32)
        out_ref[:, pl.ds(p * BLOCK, BLOCK)] = (gate * (value * (1.0 / BLOCK))).astype(jnp.bfloat16)


def inverse_blocks(spec, gate, other, wave):
    return pl.pallas_call(
        inverse_kernel,
        out_shape=jax.ShapeDtypeStruct((GROUP, CHAN * BLOCK), jnp.bfloat16),
        in_specs=[ON_CHIP] * 4,
        out_specs=ON_CHIP,
        scratch_shapes=[pltpu.VMEM((BLOCK, LANES), jnp.float32)],
        compiler_params=pltpu.CompilerParams(vmem_limit_bytes=48 * MIB),
        name="inverse_blocks",
    )(spec, gate, other, wave)


def body(projected, live_blocks, filters, skip_gain):
    exchange = partial(lax.all_to_all, split_axis=0, concat_axis=0, tiled=True)
    wave = jnp.asarray(wave_tables())
    swap = ((0, 1), (1, 0))
    got = lax.ppermute(projected, "core", swap)
    got, gain = lax.optimization_barrier((got, lane_gains(skip_gain)))
    sent, gate, send = forward_blocks(live_blocks, projected, got, filters, wave)
    other = lax.ppermute(send, "yh", swap)
    got_spec = exchange(sent.reshape(-1, 2, LANES), ("seq", "yh")).reshape(-1, LANES)
    mixed = mix_blocks(got_spec, gain)
    spec = exchange(mixed, "seq").reshape(BLOCK, LANES)
    return inverse_blocks(spec, gate, other, wave)


def solution(mesh):
    split = Mesh(mesh.devices.reshape(SEQ, 2, 2), ("seq", "yh", "core"))
    chan = ("yh", "core")
    in_specs = (P(None, None, ("seq", "yh", "core")), P("seq"), P(chan, "seq"), P(chan))
    out_specs = P(chan, "seq")
    return jax.shard_map(body, mesh=split, in_specs=in_specs, out_specs=out_specs, check_vma=False)
```

```python
from functools import partial

import jax
import jax.numpy as jnp
import ml_dtypes
import numpy as np
from jax import lax
from jax.experimental import pallas as pl
from jax.experimental.pallas import tpu as pltpu
from jax.sharding import Mesh, PartitionSpec as P

BLOCK = 1024
SEQ = 128
CHAN = 4
GROUP = 16
FREQ = BLOCK // SEQ
LANES = 128
HALF = 64
SIGNAL = 4
MESSAGE = 6
PAIR = 2 * MESSAGE
MIB = 1024 * 1024
COST = pl.CostEstimate(flops=6_000_000_000, bytes_accessed=20_000_000, transcendentals=0)
ON_CHIP = pl.BlockSpec(memory_space=pltpu.VMEM)


BASE = BLOCK // 2
QUAD = FREQ // 2


def wave_tables():
    k = np.arange(BASE, dtype=np.int64).reshape(SEQ, QUAD).T.reshape(BASE, 1)
    t = np.arange(BLOCK, dtype=np.int64)[None, :]
    angle = 2.0 * np.pi * ((2 * k + 1) * t % (4 * BLOCK)) / (4 * BLOCK)
    return np.stack([np.cos(angle), -np.sin(angle)]).astype(ml_dtypes.bfloat16)


def lane_ids(shape):
    return lax.broadcasted_iota(jnp.int32, shape, len(shape) - 1)


def row_ids(shape):
    return lax.broadcasted_iota(jnp.int32, shape, len(shape) - 2)


def swap_parts(v):
    turned = pltpu.roll(v, HALF, 1)
    return jnp.where(lane_ids(v.shape) < HALF, -turned, turned)


def gain_kernel(gain_ref, out_ref):
    out_ref[...] = jnp.concatenate([gain_ref[...]] * (LANES // GROUP), axis=1)


def lane_gains(skip_gain):
    return pl.pallas_call(
        gain_kernel,
        out_shape=jax.ShapeDtypeStruct((1, LANES), jnp.float32),
        in_specs=[ON_CHIP],
        out_specs=ON_CHIP,
        compiler_params=pltpu.CompilerParams(vmem_limit_bytes=60 * MIB),
        cost_estimate=COST,
        name="lane_gains",
    )(skip_gain.reshape(1, GROUP))


def forward_kernel(
    live_ref, own_ref, got_ref, taps_ref, wave, out_ref, gate_ref, send_ref, cols, packed
):
    high, core = lax.axis_index("yh"), lax.axis_index("core")
    side = 2 * GROUP
    piece = (GROUP, LANES)
    even = lane_ids(piece) % 2 == 0
    for part in range(2):
        rows = pl.ds(pl.multiple_of((2 * part + core) * GROUP, GROUP), GROUP)
        for blk in range(2):

            def read(i, at):
                return jnp.where(core == blk, own_ref[i, rows, at], got_ref[i, rows, at])

            to = part * HALF + blk * GROUP
            for block in range(BLOCK // LANES):
                at = pl.ds(block * LANES, LANES)
                live = live_ref[(2 * high + blk) * (BLOCK // LANES) + block].astype(jnp.float32)
                key, value = read(1, at).astype(jnp.float32), read(2, at).astype(jnp.float32)
                value = key * value * live
                cols[pl.ds(to, GROUP), at] = value.astype(jnp.bfloat16)
                value = jnp.where(even, value, -value)
                cols[pl.ds(to + side, GROUP), at] = value.astype(jnp.bfloat16)
            gate = read(0, slice(None))

            @pl.when(high == part)
            def _():
                gate_ref[blk] = gate

            @pl.when(high != part)
            def _():
                send_ref[blk] = gate

    even = lane_ids((GROUP, BLOCK)) % 2 == 0
    taps = jnp.concatenate(
        [taps_ref[:, j * BLOCK : (j + 1) * BLOCK] for j in range(CHAN)], axis=0
    )
    top = taps.astype(jnp.bfloat16).astype(jnp.float32)
    taps = jnp.concatenate([top, taps - top, top, taps - top], axis=0)
    plain = even | (row_ids((GROUP, BLOCK)) < 2 * CHAN)
    cols[pl.ds(LANES, GROUP), :] = jnp.where(plain, taps, -taps).astype(jnp.bfloat16)
    cols[pl.ds(LANES + GROUP, LANES - GROUP), :] = jnp.zeros(
        (LANES - GROUP, BLOCK), jnp.bfloat16
    )
    weights = cols[...]
    sums = []
    for i in range(2):
        sums.append(
            lax.dot_general(
                wave[i], weights, (((1,), (1,)), ((), ())), preferred_element_type=jnp.float32
            )
        )

    def put(row, value):
        packed[pl.ds(row, SEQ, stride=PAIR), :] = value

    square = (SEQ, LANES)
    lane = lane_ids(square)
    comb = jnp.zeros(square, jnp.float32)
    for i in range(QUAD):
        at = slice(i * SEQ, (i + 1) * SEQ)
        cos, sin = sums[0][at, :LANES], sums[1][at, :LANES]
        sin = jnp.where(lane % HALF < side, sin, -sin)
        put(i, jnp.where(lane < HALF, cos, pltpu.roll(sin, HALF, 1)))
        put(MESSAGE + i, jnp.where(lane < HALF, pltpu.roll(cos, HALF, 1), sin))
        for part in range(2):
            move = part * HALF + i * GROUP
            value = sums[part][at, LANES:]
            comb = comb + (pltpu.roll(value, move, 1) if move else value)
    comb = jnp.where((lane >= HALF) & ((lane // (2 * CHAN)) % 2 == 1), -comb, comb)
    comb = comb + pltpu.roll(comb, LANES - CHAN, 1)
    top = comb.astype(jnp.bfloat16).astype(jnp.float32)
    comb = jnp.where((lane // CHAN) % 2 == 0, top, pltpu.roll(comb - top, CHAN, 1))
    put(SIGNAL, jnp.where(high == 0, comb, 0.0))
    put(MESSAGE + SIGNAL, jnp.where(high == 1, comb, 0.0))
    empty = jnp.zeros(square, jnp.float32)
    put(SIGNAL + 1, empty)
    put(MESSAGE + SIGNAL + 1, empty)
    out_ref[...] = packed[pl.ds(0, SEQ * PAIR), :].astype(jnp.bfloat16)


def forward_blocks(live_blocks, own, got, taps, wave):
    gate = jax.ShapeDtypeStruct((2, GROUP, BLOCK), jnp.bfloat16)
    return pl.pallas_call(
        forward_kernel,
        out_shape=[jax.ShapeDtypeStruct((SEQ * PAIR, LANES), jnp.bfloat16), gate, gate],
        in_specs=[pl.BlockSpec(memory_space=pltpu.SMEM)] + [ON_CHIP] * 4,
        out_specs=[ON_CHIP] * 3,
        scratch_shapes=[
            pltpu.VMEM((2 * LANES, BLOCK), jnp.bfloat16),
            pltpu.VMEM(((SEQ + 1) * PAIR, LANES), jnp.float32),
        ],
        compiler_params=pltpu.CompilerParams(vmem_limit_bytes=48 * MIB),
        name="forward_blocks",
    )(live_blocks, own, got, taps, wave)


def mix_kernel(in_ref, gain_ref, out_ref, spread, wide, matrix):
    spread[pl.ds(0, SEQ * PAIR), :] = in_ref[...].astype(jnp.float32)
    square = (SEQ, LANES)
    row, lane = row_ids(square), lane_ids(square)

    def take(at):
        return spread[pl.ds(at, SEQ, stride=PAIR), :]

    comb = take(SIGNAL) + take(MESSAGE + SIGNAL)
    negate = jnp.where((row + lane) % SEQ == 0, 1.0, 0.0).astype(jnp.bfloat16)
    turned = jnp.dot(comb.T.astype(jnp.bfloat16), negate, preferred_element_type=jnp.float32)
    turned = turned + pltpu.roll(turned, LANES - CHAN, 0)
    late = jnp.where(lane == 0, 0.0, pltpu.roll(turned, SEQ - 1, 1))
    before = jnp.where(
        row % CHAN == 0, pltpu.roll(late, LANES - CHAN + 1, 0), pltpu.roll(turned, 1, 0)
    )
    half_row = row_ids((HALF, LANES))
    flip = (half_row // (4 * CHAN) + half_row // (2 * CHAN)) % 2 == 1
    before = jnp.where(jnp.concatenate([flip, flip], axis=0), -before, before)
    spec = (turned[:HALF] - before[HALF:], turned[HALF:] + before[:HALF])
    causal = lane <= row
    gain = gain_ref[...]
    low_lane = lane % HALF < 2 * GROUP
    signals, rows = [], []
    for k in range(FREQ):
        digit, mirror = k // 2, k % 2
        low, high = take(digit), take(MESSAGE + digit)
        if mirror == 0:
            signal = jnp.where(low_lane, low, pltpu.roll(high, 2 * GROUP, 1))
        else:
            signal = jnp.where(low_lane, pltpu.roll(low, LANES - 2 * GROUP, 1), high)
        late = jnp.where(row == 0, 0.0, pltpu.roll(signal, 1, 0))
        signals.append(signal)
        rows.append(jnp.concatenate([signal, late], axis=1).astype(jnp.bfloat16))
    rows = jnp.concatenate(rows, axis=0)
    shape = (2 * LANES, (CHAN - 1) * LANES)
    source, target = row_ids(shape), lane_ids(shape)
    place = source % HALF + GROUP * (target // LANES + 1) - jnp.where(source < LANES, 0, HALF)
    same_part = (source // HALF) % 2 == (target // HALF) % 2
    shifts = jnp.where(same_part & (place == target % HALF), 1.0, 0.0).astype(jnp.bfloat16)
    moved = jnp.dot(rows, shifts, preferred_element_type=jnp.float32).astype(jnp.bfloat16)
    for k in range(FREQ):
        digit, mirror = k // 2, k % 2
        base = digit * 4 * CHAN + mirror * 2 * CHAN
        for q in range(CHAN):
            for part in range(2):
                line = spec[part][base + q : base + q + 1, :]
                tall = jnp.broadcast_to(line, square)
                toeplitz = pltpu.roll(tall, 0, 1, stride=1, stride_axis=0)
                toeplitz = jnp.where(causal, toeplitz, 0.0)
                matrix[pl.ds(part * SEQ, SEQ), pl.ds(q * SEQ, SEQ)] = toeplitz.astype(jnp.bfloat16)
        signal = signals[k]
        at = slice(k * SEQ, (k + 1) * SEQ)
        shifted = [rows[at, :LANES]]
        shifted += [moved[at, q * LANES : (q + 1) * LANES] for q in range(CHAN - 1)]
        parts = jnp.dot(
            matrix[...], jnp.concatenate(shifted, axis=0), preferred_element_type=jnp.float32
        )
        mixed = parts[:SEQ, :] + swap_parts(parts[SEQ:, :]) + gain * signal
        if mirror == 0:
            first = mixed
            continue
        plus, minus = first + mixed, first - mixed
        wide[:, digit, :] = jnp.where(lane < HALF, plus, minus)
        wide[:, QUAD + digit, :] = jnp.where(lane < HALF, minus, plus)
    out_ref[...] = wide[...].astype(jnp.bfloat16)


def mix_blocks(received, gain):
    return pl.pallas_call(
        mix_kernel,
        out_shape=jax.ShapeDtypeStruct((SEQ, FREQ, LANES), jnp.bfloat16),
        in_specs=[ON_CHIP, ON_CHIP],
        out_specs=ON_CHIP,
        scratch_shapes=[
            pltpu.VMEM(((SEQ + 1) * PAIR, LANES), jnp.float32),
            pltpu.VMEM((SEQ, FREQ, LANES), jnp.float32),
            pltpu.VMEM((2 * SEQ, CHAN * SEQ), jnp.bfloat16),
        ],
        compiler_params=pltpu.CompilerParams(vmem_limit_bytes=48 * MIB),
        cost_estimate=COST,
        name="mix_blocks",
    )(received, gain)


def inverse_kernel(spec_ref, gate_ref, other_ref, wave, out_ref, plain):
    plain[pl.ds(0, BLOCK), :] = spec_ref[...].astype(jnp.float32)
    sides = [
        [plain[pl.ds(part * QUAD + i, SEQ, stride=FREQ), :].T for i in range(QUAD)]
        for part in range(2)
    ]
    sides = [jnp.concatenate(side, axis=1).astype(jnp.bfloat16) for side in sides]
    total = None
    for part in range(2):
        lines = [side[part * HALF : (part + 1) * HALF, :] for side in sides]
        term = jnp.dot(
            jnp.concatenate(lines, axis=0), wave[part], preferred_element_type=jnp.float32
        )
        total = term if total is None else total + term
    high = lax.axis_index("yh")
    even = lane_ids((GROUP, BLOCK)) % 2 == 0
    for p in range(CHAN):
        at = p * GROUP
        value = jnp.where(
            even, total[at : at + GROUP, :], total[HALF + at : HALF + at + GROUP, :]
        )
        gate = jnp.where(high == p // 2, gate_ref[p % 2], other_ref[p % 2]).astype(jnp.float32)
        out_ref[:, pl.ds(p * BLOCK, BLOCK)] = (gate * (value * (1.0 / BLOCK))).astype(jnp.bfloat16)


def inverse_blocks(spec, gate, other, wave):
    return pl.pallas_call(
        inverse_kernel,
        out_shape=jax.ShapeDtypeStruct((GROUP, CHAN * BLOCK), jnp.bfloat16),
        in_specs=[ON_CHIP] * 4,
        out_specs=ON_CHIP,
        scratch_shapes=[pltpu.VMEM((BLOCK + FREQ, LANES), jnp.float32)],
        compiler_params=pltpu.CompilerParams(vmem_limit_bytes=48 * MIB),
        name="inverse_blocks",
    )(spec, gate, other, wave)


def body(projected, live_blocks, filters, skip_gain):
    exchange = partial(lax.all_to_all, split_axis=0, concat_axis=0, tiled=True)
    wave = jnp.asarray(wave_tables())
    swap = ((0, 1), (1, 0))
    got = lax.ppermute(projected, "core", swap)
    got, gain = lax.optimization_barrier((got, lane_gains(skip_gain)))
    sent, gate, send = forward_blocks(live_blocks, projected, got, filters, wave)
    other = lax.ppermute(send, "yh", swap)
    got_spec = exchange(sent.reshape(-1, 2, LANES), ("seq", "yh")).reshape(-1, LANES)
    mixed = mix_blocks(got_spec, gain)
    spec = exchange(mixed, "seq").reshape(BLOCK, LANES)
    return inverse_blocks(spec, gate, other, wave)


def solution(mesh):
    split = Mesh(mesh.devices.reshape(SEQ, 2, 2), ("seq", "yh", "core"))
    chan = ("yh", "core")
    in_specs = (P(None, None, ("seq", "yh", "core")), P("seq"), P(chan, "seq"), P(chan))
    out_specs = P(chan, "seq")
    return jax.shard_map(body, mesh=split, in_specs=in_specs, out_specs=out_specs, check_vma=False)
```

```python
from functools import partial

import jax
import jax.numpy as jnp
import ml_dtypes
import numpy as np
from jax import lax
from jax.experimental import pallas as pl
from jax.experimental.pallas import tpu as pltpu
from jax.sharding import Mesh, PartitionSpec as P

BLOCK = 1024
SEQ = 128
CHAN = 4
GROUP = 16
FREQ = BLOCK // SEQ
LANES = 128
HALF = 64
SIGNAL = 4
MESSAGE = 6
PAIR = 2 * MESSAGE
ANSWER = FREQ + 2
MIB = 1024 * 1024
COST = pl.CostEstimate(flops=6_000_000_000, bytes_accessed=20_000_000, transcendentals=0)
ON_CHIP = pl.BlockSpec(memory_space=pltpu.VMEM)


BASE = BLOCK // 2
QUAD = FREQ // 2


def wave_tables():
    k = np.arange(BASE, dtype=np.int64).reshape(SEQ, QUAD).T.reshape(BASE, 1)
    t = np.arange(BLOCK, dtype=np.int64)[None, :]
    angle = 2.0 * np.pi * ((2 * k + 1) * t % (4 * BLOCK)) / (4 * BLOCK)
    return np.stack([np.cos(angle), -np.sin(angle)]).astype(ml_dtypes.bfloat16)


def lane_ids(shape):
    return lax.broadcasted_iota(jnp.int32, shape, len(shape) - 1)


def row_ids(shape):
    return lax.broadcasted_iota(jnp.int32, shape, len(shape) - 2)


def swap_parts(v):
    turned = pltpu.roll(v, HALF, 1)
    return jnp.where(lane_ids(v.shape) < HALF, -turned, turned)


def gain_kernel(gain_ref, out_ref):
    out_ref[...] = jnp.concatenate([gain_ref[...]] * (LANES // GROUP), axis=1)


def lane_gains(skip_gain):
    return pl.pallas_call(
        gain_kernel,
        out_shape=jax.ShapeDtypeStruct((1, LANES), jnp.float32),
        in_specs=[ON_CHIP],
        out_specs=ON_CHIP,
        compiler_params=pltpu.CompilerParams(vmem_limit_bytes=60 * MIB),
        cost_estimate=COST,
        name="lane_gains",
    )(skip_gain.reshape(1, GROUP))


def gate_pieces(blk):
    return [(i, i % 2, blk * QUAD + i // 2) for i in range(BLOCK // LANES)]


def forward_kernel(
    live_ref, own_ref, got_ref, taps_ref, wave, out_ref, gate_ref, cols, packed, parcel
):
    high, core = lax.axis_index("yh"), lax.axis_index("core")
    side = 2 * GROUP
    piece = (GROUP, LANES)
    even = lane_ids(piece) % 2 == 0
    for part in range(2):
        rows = pl.ds(pl.multiple_of((2 * part + core) * GROUP, GROUP), GROUP)
        for blk in range(2):

            def read(i, at):
                return jnp.where(core == blk, own_ref[i, rows, at], got_ref[i, rows, at])

            to = part * HALF + blk * GROUP
            for block in range(BLOCK // LANES):
                at = pl.ds(block * LANES, LANES)
                live = live_ref[(2 * high + blk) * (BLOCK // LANES) + block].astype(jnp.float32)
                key, value = read(1, at).astype(jnp.float32), read(2, at).astype(jnp.float32)
                value = key * value * live
                cols[pl.ds(to, GROUP), at] = value.astype(jnp.bfloat16)
                value = jnp.where(even, value, -value)
                cols[pl.ds(to + side, GROUP), at] = value.astype(jnp.bfloat16)
            gate = read(0, slice(None))

            @pl.when(high == part)
            def _():
                gate_ref[blk] = gate

            @pl.when(high != part)
            def _():
                for piece_at, row, number in gate_pieces(blk):
                    at = pl.ds(piece_at * LANES, LANES)
                    value = read(0, at).astype(jnp.float32)
                    parcel[row, pl.ds(number, GROUP, stride=FREQ), :] = value

    even = lane_ids((GROUP, BLOCK)) % 2 == 0
    taps = jnp.concatenate(
        [taps_ref[:, j * BLOCK : (j + 1) * BLOCK] for j in range(CHAN)], axis=0
    )
    top = taps.astype(jnp.bfloat16).astype(jnp.float32)
    taps = jnp.concatenate([top, taps - top, top, taps - top], axis=0)
    plain = even | (row_ids((GROUP, BLOCK)) < 2 * CHAN)
    cols[pl.ds(LANES, GROUP), :] = jnp.where(plain, taps, -taps).astype(jnp.bfloat16)
    cols[pl.ds(LANES + GROUP, LANES - GROUP), :] = jnp.zeros(
        (LANES - GROUP, BLOCK), jnp.bfloat16
    )
    weights = cols[...]
    sums = []
    for i in range(2):
        sums.append(
            lax.dot_general(
                wave[i], weights, (((1,), (1,)), ((), ())), preferred_element_type=jnp.float32
            )
        )

    def put(row, value):
        packed[pl.ds(row, SEQ, stride=PAIR), :] = value

    square = (SEQ, LANES)
    lane = lane_ids(square)
    comb = jnp.zeros(square, jnp.float32)
    for i in range(QUAD):
        at = slice(i * SEQ, (i + 1) * SEQ)
        cos, sin = sums[0][at, :LANES], sums[1][at, :LANES]
        sin = jnp.where(lane % HALF < side, sin, -sin)
        put(i, jnp.where(lane < HALF, cos, pltpu.roll(sin, HALF, 1)))
        put(MESSAGE + i, jnp.where(lane < HALF, pltpu.roll(cos, HALF, 1), sin))
        for part in range(2):
            move = part * HALF + i * GROUP
            value = sums[part][at, LANES:]
            comb = comb + (pltpu.roll(value, move, 1) if move else value)
    comb = jnp.where((lane >= HALF) & ((lane // (2 * CHAN)) % 2 == 1), -comb, comb)
    comb = comb + pltpu.roll(comb, LANES - CHAN, 1)
    top = comb.astype(jnp.bfloat16).astype(jnp.float32)
    comb = jnp.where((lane // CHAN) % 2 == 0, top, pltpu.roll(comb - top, CHAN, 1))
    for group in range(2):
        at = group * MESSAGE + SIGNAL
        put(at, jnp.where(high == group, comb, parcel[0, pl.ds(0, SEQ), :]))
        put(at + 1, jnp.where(high == group, 0.0, parcel[1, pl.ds(0, SEQ), :]))
    out_ref[...] = packed[pl.ds(0, SEQ * PAIR), :].astype(jnp.bfloat16)


def forward_blocks(live_blocks, own, got, taps, wave):
    gate = jax.ShapeDtypeStruct((2, GROUP, BLOCK), jnp.bfloat16)
    return pl.pallas_call(
        forward_kernel,
        out_shape=[jax.ShapeDtypeStruct((SEQ * PAIR, LANES), jnp.bfloat16), gate],
        in_specs=[pl.BlockSpec(memory_space=pltpu.SMEM)] + [ON_CHIP] * 4,
        out_specs=[ON_CHIP] * 2,
        scratch_shapes=[
            pltpu.VMEM((2 * LANES, BLOCK), jnp.bfloat16),
            pltpu.VMEM(((SEQ + 1) * PAIR, LANES), jnp.float32),
            pltpu.VMEM((2, SEQ + FREQ, LANES), jnp.float32),
        ],
        compiler_params=pltpu.CompilerParams(vmem_limit_bytes=48 * MIB),
        name="forward_blocks",
    )(live_blocks, own, got, taps, wave)


def mix_kernel(in_ref, gain_ref, out_ref, spread, wide, matrix):
    spread[pl.ds(0, SEQ * PAIR), :] = in_ref[...].astype(jnp.float32)
    square = (SEQ, LANES)
    row, lane = row_ids(square), lane_ids(square)

    def take(at):
        return spread[pl.ds(at, SEQ, stride=PAIR), :]

    def put(row, value):
        wide[pl.ds(row, SEQ, stride=ANSWER), :] = value

    own = lax.axis_index("yh")
    extra = [take(at + SIGNAL) for at in (0, MESSAGE)]
    comb = jnp.where(own == 0, extra[0], extra[1])
    negate = jnp.where((row + lane) % SEQ == 0, 1.0, 0.0).astype(jnp.bfloat16)
    turned = jnp.dot(comb.T.astype(jnp.bfloat16), negate, preferred_element_type=jnp.float32)
    turned = turned + pltpu.roll(turned, LANES - CHAN, 0)
    late = jnp.where(lane == 0, 0.0, pltpu.roll(turned, SEQ - 1, 1))
    before = jnp.where(
        row % CHAN == 0, pltpu.roll(late, LANES - CHAN + 1, 0), pltpu.roll(turned, 1, 0)
    )
    half_row = row_ids((HALF, LANES))
    flip = (half_row // (4 * CHAN) + half_row // (2 * CHAN)) % 2 == 1
    before = jnp.where(jnp.concatenate([flip, flip], axis=0), -before, before)
    spec = (turned[:HALF] - before[HALF:], turned[HALF:] + before[:HALF])
    causal = lane <= row
    gain = gain_ref[...]
    low_lane = lane % HALF < 2 * GROUP
    signals, rows = [], []
    for k in range(FREQ):
        digit, mirror = k // 2, k % 2
        low, high = take(digit), take(MESSAGE + digit)
        if mirror == 0:
            signal = jnp.where(low_lane, low, pltpu.roll(high, 2 * GROUP, 1))
        else:
            signal = jnp.where(low_lane, pltpu.roll(low, LANES - 2 * GROUP, 1), high)
        late = jnp.where(row == 0, 0.0, pltpu.roll(signal, 1, 0))
        signals.append(signal)
        rows.append(jnp.concatenate([signal, late], axis=1).astype(jnp.bfloat16))
    rows = jnp.concatenate(rows, axis=0)
    shape = (2 * LANES, (CHAN - 1) * LANES)
    source, target = row_ids(shape), lane_ids(shape)
    place = source % HALF + GROUP * (target // LANES + 1) - jnp.where(source < LANES, 0, HALF)
    same_part = (source // HALF) % 2 == (target // HALF) % 2
    shifts = jnp.where(same_part & (place == target % HALF), 1.0, 0.0).astype(jnp.bfloat16)
    moved = jnp.dot(rows, shifts, preferred_element_type=jnp.float32).astype(jnp.bfloat16)
    for k in range(FREQ):
        digit, mirror = k // 2, k % 2
        base = digit * 4 * CHAN + mirror * 2 * CHAN
        for q in range(CHAN):
            for part in range(2):
                line = spec[part][base + q : base + q + 1, :]
                tall = jnp.broadcast_to(line, square)
                toeplitz = pltpu.roll(tall, 0, 1, stride=1, stride_axis=0)
                toeplitz = jnp.where(causal, toeplitz, 0.0)
                matrix[pl.ds(part * SEQ, SEQ), pl.ds(q * SEQ, SEQ)] = toeplitz.astype(jnp.bfloat16)
        signal = signals[k]
        at = slice(k * SEQ, (k + 1) * SEQ)
        shifted = [rows[at, :LANES]]
        shifted += [moved[at, q * LANES : (q + 1) * LANES] for q in range(CHAN - 1)]
        parts = jnp.dot(
            matrix[...], jnp.concatenate(shifted, axis=0), preferred_element_type=jnp.float32
        )
        mixed = parts[:SEQ, :] + swap_parts(parts[SEQ:, :]) + gain * signal
        if mirror == 0:
            first = mixed
            continue
        plus, minus = first + mixed, first - mixed
        put(digit, jnp.where(lane < HALF, plus, minus))
        put(QUAD + digit, jnp.where(lane < HALF, minus, plus))
    put(FREQ, jnp.where(own == 0, extra[1], extra[0]))
    put(FREQ + 1, jnp.where(own == 0, take(PAIR - 1), take(MESSAGE - 1)))
    out_ref[...] = wide[pl.ds(0, SEQ * ANSWER), :].astype(jnp.bfloat16)


def mix_blocks(received, gain):
    return pl.pallas_call(
        mix_kernel,
        out_shape=jax.ShapeDtypeStruct((SEQ * ANSWER, LANES), jnp.bfloat16),
        in_specs=[ON_CHIP, ON_CHIP],
        out_specs=ON_CHIP,
        scratch_shapes=[
            pltpu.VMEM(((SEQ + 1) * PAIR, LANES), jnp.float32),
            pltpu.VMEM(((SEQ + 1) * ANSWER, LANES), jnp.float32),
            pltpu.VMEM((2 * SEQ, CHAN * SEQ), jnp.bfloat16),
        ],
        compiler_params=pltpu.CompilerParams(vmem_limit_bytes=48 * MIB),
        cost_estimate=COST,
        name="mix_blocks",
    )(received, gain)


def inverse_kernel(spec_ref, gate_ref, wave, out_ref, plain):
    plain[pl.ds(0, SEQ * ANSWER), :] = spec_ref[...].astype(jnp.float32)
    sides = [
        [plain[pl.ds(part * QUAD + i, SEQ, stride=ANSWER), :].T for i in range(QUAD)]
        for part in range(2)
    ]
    sides = [jnp.concatenate(side, axis=1).astype(jnp.bfloat16) for side in sides]
    total = None
    for part in range(2):
        lines = [side[part * HALF : (part + 1) * HALF, :] for side in sides]
        term = jnp.dot(
            jnp.concatenate(lines, axis=0), wave[part], preferred_element_type=jnp.float32
        )
        total = term if total is None else total + term
    high = lax.axis_index("yh")
    even = lane_ids((GROUP, BLOCK)) % 2 == 0
    for p in range(CHAN):
        at = p * GROUP
        value = jnp.where(
            even, total[at : at + GROUP, :], total[HALF + at : HALF + at + GROUP, :]
        )
        other = [
            plain[pl.ds(number * ANSWER + FREQ + row, GROUP, stride=FREQ * ANSWER), :]
            for _, row, number in gate_pieces(p % 2)
        ]
        other = jnp.concatenate(other, axis=1)
        gate = jnp.where(high == p // 2, gate_ref[p % 2].astype(jnp.float32), other)
        out_ref[:, pl.ds(p * BLOCK, BLOCK)] = (gate * (value * (1.0 / BLOCK))).astype(jnp.bfloat16)


def inverse_blocks(spec, gate, wave):
    return pl.pallas_call(
        inverse_kernel,
        out_shape=jax.ShapeDtypeStruct((GROUP, CHAN * BLOCK), jnp.bfloat16),
        in_specs=[ON_CHIP] * 3,
        out_specs=ON_CHIP,
        scratch_shapes=[pltpu.VMEM(((SEQ + FREQ) * ANSWER, LANES), jnp.float32)],
        compiler_params=pltpu.CompilerParams(vmem_limit_bytes=48 * MIB),
        name="inverse_blocks",
    )(spec, gate, wave)


def body(projected, live_blocks, filters, skip_gain):
    exchange = partial(lax.all_to_all, split_axis=0, concat_axis=0, tiled=True)
    wave = jnp.asarray(wave_tables())
    swap = ((0, 1), (1, 0))
    got = lax.ppermute(projected, "core", swap)
    got, gain = lax.optimization_barrier((got, lane_gains(skip_gain)))
    sent, gate = forward_blocks(live_blocks, projected, got, filters, wave)
    got_spec = exchange(sent.reshape(-1, 2, LANES), ("seq", "yh")).reshape(-1, LANES)
    mixed = mix_blocks(got_spec, gain)
    spec = exchange(mixed.reshape(-1, 2, LANES), "seq").reshape(-1, LANES)
    return inverse_blocks(spec, gate, wave)


def solution(mesh):
    split = Mesh(mesh.devices.reshape(SEQ, 2, 2), ("seq", "yh", "core"))
    chan = ("yh", "core")
    in_specs = (P(None, None, ("seq", "yh", "core")), P("seq"), P(chan, "seq"), P(chan))
    out_specs = P(chan, "seq")
    return jax.shard_map(body, mesh=split, in_specs=in_specs, out_specs=out_specs, check_vma=False)
```

```python
from functools import partial

import jax
import jax.numpy as jnp
import ml_dtypes
import numpy as np
from jax import lax
from jax.experimental import pallas as pl
from jax.experimental.pallas import tpu as pltpu
from jax.sharding import Mesh, PartitionSpec as P

BLOCK = 1024
SEQ = 128
CHAN = 4
GROUP = 16
FREQ = BLOCK // SEQ
LANES = 128
HALF = 64
SIGNAL = 4
MESSAGE = 6
PAIR = 2 * MESSAGE
ANSWER = FREQ + 2
MIB = 1024 * 1024
COST = pl.CostEstimate(flops=6_000_000_000, bytes_accessed=20_000_000, transcendentals=0)
ON_CHIP = pl.BlockSpec(memory_space=pltpu.VMEM)


BASE = BLOCK // 2
QUAD = FREQ // 2


def wave_tables():
    k = np.arange(BASE, dtype=np.int64).reshape(SEQ, QUAD).T.reshape(BASE, 1)
    t = np.arange(BLOCK, dtype=np.int64)[None, :]
    angle = 2.0 * np.pi * ((2 * k + 1) * t % (4 * BLOCK)) / (4 * BLOCK)
    return np.stack([np.cos(angle), -np.sin(angle)]).astype(ml_dtypes.bfloat16)


def lane_ids(shape):
    return lax.broadcasted_iota(jnp.int32, shape, len(shape) - 1)


def row_ids(shape):
    return lax.broadcasted_iota(jnp.int32, shape, len(shape) - 2)


def swap_parts(v):
    turned = pltpu.roll(v, HALF, 1)
    return jnp.where(lane_ids(v.shape) < HALF, -turned, turned)


def gain_kernel(gain_ref, out_ref):
    out_ref[...] = jnp.concatenate([gain_ref[...]] * (LANES // GROUP), axis=1)


def lane_gains(skip_gain):
    return pl.pallas_call(
        gain_kernel,
        out_shape=jax.ShapeDtypeStruct((1, LANES), jnp.float32),
        in_specs=[ON_CHIP],
        out_specs=ON_CHIP,
        compiler_params=pltpu.CompilerParams(vmem_limit_bytes=60 * MIB),
        cost_estimate=COST,
        name="lane_gains",
    )(skip_gain.reshape(1, GROUP))


def gate_pieces(blk):
    return [(i, i % 2, blk * QUAD + i // 2) for i in range(BLOCK // LANES)]


def forward_kernel(
    live_ref, own_ref, got_ref, taps_ref, wave, out_ref, gate_ref, cols, packed, parcel
):
    high, core = lax.axis_index("yh"), lax.axis_index("core")
    lives = live_ref[...].astype(jnp.float32)
    places = lane_ids(lives.shape)
    side = 2 * GROUP
    piece = (GROUP, LANES)
    even = lane_ids(piece) % 2 == 0
    for part in range(2):
        rows = pl.ds(pl.multiple_of((2 * part + core) * GROUP, GROUP), GROUP)
        for blk in range(2):

            def read(i, at):
                return jnp.where(core == blk, own_ref[i, rows, at], got_ref[i, rows, at])

            to = part * HALF + blk * GROUP
            for block in range(BLOCK // LANES):
                at = pl.ds(block * LANES, LANES)
                number = (2 * high + blk) * (BLOCK // LANES) + block
                live = jnp.sum(jnp.where(places == number, lives, 0.0), axis=1, keepdims=True)
                key, value = read(1, at).astype(jnp.float32), read(2, at).astype(jnp.float32)
                value = key * value * live
                cols[pl.ds(to, GROUP), at] = value.astype(jnp.bfloat16)
                value = jnp.where(even, value, -value)
                cols[pl.ds(to + side, GROUP), at] = value.astype(jnp.bfloat16)
            gate = read(0, slice(None))

            @pl.when(high == part)
            def _():
                gate_ref[blk] = gate

            @pl.when(high != part)
            def _():
                for piece_at, row, number in gate_pieces(blk):
                    at = pl.ds(piece_at * LANES, LANES)
                    value = read(0, at).astype(jnp.float32)
                    parcel[row, pl.ds(number, GROUP, stride=FREQ), :] = value

    even = lane_ids((GROUP, BLOCK)) % 2 == 0
    taps = jnp.concatenate(
        [taps_ref[:, j * BLOCK : (j + 1) * BLOCK] for j in range(CHAN)], axis=0
    )
    top = taps.astype(jnp.bfloat16).astype(jnp.float32)
    taps = jnp.concatenate([top, taps - top, top, taps - top], axis=0)
    plain = even | (row_ids((GROUP, BLOCK)) < 2 * CHAN)
    cols[pl.ds(LANES, GROUP), :] = jnp.where(plain, taps, -taps).astype(jnp.bfloat16)
    cols[pl.ds(LANES + GROUP, LANES - GROUP), :] = jnp.zeros(
        (LANES - GROUP, BLOCK), jnp.bfloat16
    )
    weights = cols[...]
    sums = []
    for i in range(2):
        sums.append(
            lax.dot_general(
                wave[i], weights, (((1,), (1,)), ((), ())), preferred_element_type=jnp.float32
            )
        )

    def put(row, value):
        packed[pl.ds(row, SEQ, stride=PAIR), :] = value

    square = (SEQ, LANES)
    lane = lane_ids(square)
    comb = jnp.zeros(square, jnp.float32)
    for i in range(QUAD):
        at = slice(i * SEQ, (i + 1) * SEQ)
        cos, sin = sums[0][at, :LANES], sums[1][at, :LANES]
        sin = jnp.where(lane % HALF < side, sin, -sin)
        put(i, jnp.where(lane < HALF, cos, pltpu.roll(sin, HALF, 1)))
        put(MESSAGE + i, jnp.where(lane < HALF, pltpu.roll(cos, HALF, 1), sin))
        for part in range(2):
            move = part * HALF + i * GROUP
            value = sums[part][at, LANES:]
            comb = comb + (pltpu.roll(value, move, 1) if move else value)
    comb = jnp.where((lane >= HALF) & ((lane // (2 * CHAN)) % 2 == 1), -comb, comb)
    comb = comb + pltpu.roll(comb, LANES - CHAN, 1)
    top = comb.astype(jnp.bfloat16).astype(jnp.float32)
    comb = jnp.where((lane // CHAN) % 2 == 0, top, pltpu.roll(comb - top, CHAN, 1))
    for group in range(2):
        at = group * MESSAGE + SIGNAL
        put(at, jnp.where(high == group, comb, parcel[0, pl.ds(0, SEQ), :]))
        put(at + 1, jnp.where(high == group, 0.0, parcel[1, pl.ds(0, SEQ), :]))
    out_ref[...] = packed[pl.ds(0, SEQ * PAIR), :].astype(jnp.bfloat16)


def forward_blocks(live_blocks, own, got, taps, wave):
    gate = jax.ShapeDtypeStruct((2, GROUP, BLOCK), jnp.bfloat16)
    return pl.pallas_call(
        forward_kernel,
        out_shape=[jax.ShapeDtypeStruct((SEQ * PAIR, LANES), jnp.bfloat16), gate],
        in_specs=[ON_CHIP] * 5,
        out_specs=[ON_CHIP] * 2,
        scratch_shapes=[
            pltpu.VMEM((2 * LANES, BLOCK), jnp.bfloat16),
            pltpu.VMEM(((SEQ + 1) * PAIR, LANES), jnp.float32),
            pltpu.VMEM((2, SEQ + FREQ, LANES), jnp.float32),
        ],
        compiler_params=pltpu.CompilerParams(vmem_limit_bytes=48 * MIB),
        name="forward_blocks",
    )(live_blocks.reshape(1, -1), own, got, taps, wave)


def mix_kernel(in_ref, gain_ref, out_ref, spread, wide):
    spread[pl.ds(0, SEQ * PAIR), :] = in_ref[...].astype(jnp.float32)
    square = (SEQ, LANES)
    row, lane = row_ids(square), lane_ids(square)

    def take(at):
        return spread[pl.ds(at, SEQ, stride=PAIR), :]

    def put(row, value):
        wide[pl.ds(row, SEQ, stride=ANSWER), :] = value

    own = lax.axis_index("yh")
    extra = [take(at + SIGNAL) for at in (0, MESSAGE)]
    comb = jnp.where(own == 0, extra[0], extra[1])
    negate = jnp.where((row + lane) % SEQ == 0, 1.0, 0.0).astype(jnp.bfloat16)
    turned = jnp.dot(comb.T.astype(jnp.bfloat16), negate, preferred_element_type=jnp.float32)
    turned = turned + pltpu.roll(turned, LANES - CHAN, 0)
    late = jnp.where(lane == 0, 0.0, pltpu.roll(turned, SEQ - 1, 1))
    before = jnp.where(
        row % CHAN == 0, pltpu.roll(late, LANES - CHAN + 1, 0), pltpu.roll(turned, 1, 0)
    )
    half_row = row_ids((HALF, LANES))
    flip = (half_row // (4 * CHAN) + half_row // (2 * CHAN)) % 2 == 1
    before = jnp.where(jnp.concatenate([flip, flip], axis=0), -before, before)
    spec = (turned[:HALF] - before[HALF:], turned[HALF:] + before[:HALF])
    causal = lane <= row
    gain = gain_ref[...]
    low_lane = lane % HALF < 2 * GROUP
    signals, rows = [], []
    for k in range(FREQ):
        digit, mirror = k // 2, k % 2
        low, high = take(digit), take(MESSAGE + digit)
        if mirror == 0:
            signal = jnp.where(low_lane, low, pltpu.roll(high, 2 * GROUP, 1))
        else:
            signal = jnp.where(low_lane, pltpu.roll(low, LANES - 2 * GROUP, 1), high)
        late = jnp.where(row == 0, 0.0, pltpu.roll(signal, 1, 0))
        signals.append(signal)
        rows.append(jnp.concatenate([signal, late], axis=1).astype(jnp.bfloat16))
    rows = jnp.concatenate(rows, axis=0)
    shape = (2 * LANES, (CHAN - 1) * LANES)
    source, target = row_ids(shape), lane_ids(shape)
    place = source % HALF + GROUP * (target // LANES + 1) - jnp.where(source < LANES, 0, HALF)
    same_part = (source // HALF) % 2 == (target // HALF) % 2
    shifts = jnp.where(same_part & (place == target % HALF), 1.0, 0.0).astype(jnp.bfloat16)
    moved = jnp.dot(rows, shifts, preferred_element_type=jnp.float32).astype(jnp.bfloat16)
    for k in range(FREQ):
        digit, mirror = k // 2, k % 2
        base = digit * 4 * CHAN + mirror * 2 * CHAN
        tiles = ([], [])
        for q in range(CHAN):
            for part in range(2):
                line = spec[part][base + q : base + q + 1, :]
                tall = jnp.broadcast_to(line, square)
                toeplitz = pltpu.roll(tall, 0, 1, stride=1, stride_axis=0)
                toeplitz = jnp.where(causal, toeplitz, 0.0)
                tiles[part].append(toeplitz.astype(jnp.bfloat16))
        signal = signals[k]
        at = slice(k * SEQ, (k + 1) * SEQ)
        shifted = [rows[at, :LANES]]
        shifted += [moved[at, q * LANES : (q + 1) * LANES] for q in range(CHAN - 1)]
        matrix = jnp.concatenate([jnp.concatenate(line, axis=1) for line in tiles], axis=0)
        parts = jnp.dot(
            matrix, jnp.concatenate(shifted, axis=0), preferred_element_type=jnp.float32
        )
        mixed = parts[:SEQ, :] + swap_parts(parts[SEQ:, :]) + gain * signal
        if mirror == 0:
            first = mixed
            continue
        plus, minus = first + mixed, first - mixed
        put(digit, jnp.where(lane < HALF, plus, minus))
        put(QUAD + digit, jnp.where(lane < HALF, minus, plus))
    put(FREQ, jnp.where(own == 0, extra[1], extra[0]))
    put(FREQ + 1, jnp.where(own == 0, take(PAIR - 1), take(MESSAGE - 1)))
    out_ref[...] = wide[pl.ds(0, SEQ * ANSWER), :].astype(jnp.bfloat16)


def mix_blocks(received, gain):
    return pl.pallas_call(
        mix_kernel,
        out_shape=jax.ShapeDtypeStruct((SEQ * ANSWER, LANES), jnp.bfloat16),
        in_specs=[ON_CHIP, ON_CHIP],
        out_specs=ON_CHIP,
        scratch_shapes=[
            pltpu.VMEM(((SEQ + 1) * PAIR, LANES), jnp.float32),
            pltpu.VMEM(((SEQ + 1) * ANSWER, LANES), jnp.float32),
        ],
        compiler_params=pltpu.CompilerParams(vmem_limit_bytes=48 * MIB),
        cost_estimate=COST,
        name="mix_blocks",
    )(received, gain)


def inverse_kernel(spec_ref, gate_ref, wave, out_ref, plain):
    plain[pl.ds(0, SEQ * ANSWER), :] = spec_ref[...].astype(jnp.float32)
    sides = [
        [plain[pl.ds(part * QUAD + i, SEQ, stride=ANSWER), :].T for i in range(QUAD)]
        for part in range(2)
    ]
    sides = [jnp.concatenate(side, axis=1).astype(jnp.bfloat16) for side in sides]
    total = None
    for part in range(2):
        lines = [side[part * HALF : (part + 1) * HALF, :] for side in sides]
        term = jnp.dot(
            jnp.concatenate(lines, axis=0), wave[part], preferred_element_type=jnp.float32
        )
        total = term if total is None else total + term
    high = lax.axis_index("yh")
    even = lane_ids((GROUP, BLOCK)) % 2 == 0
    for p in range(CHAN):
        at = p * GROUP
        value = jnp.where(
            even, total[at : at + GROUP, :], total[HALF + at : HALF + at + GROUP, :]
        )
        other = [
            plain[pl.ds(number * ANSWER + FREQ + row, GROUP, stride=FREQ * ANSWER), :]
            for _, row, number in gate_pieces(p % 2)
        ]
        other = jnp.concatenate(other, axis=1)
        gate = jnp.where(high == p // 2, gate_ref[p % 2].astype(jnp.float32), other)
        out_ref[:, pl.ds(p * BLOCK, BLOCK)] = (gate * (value * (1.0 / BLOCK))).astype(jnp.bfloat16)


def inverse_blocks(spec, gate, wave):
    return pl.pallas_call(
        inverse_kernel,
        out_shape=jax.ShapeDtypeStruct((GROUP, CHAN * BLOCK), jnp.bfloat16),
        in_specs=[ON_CHIP] * 3,
        out_specs=ON_CHIP,
        scratch_shapes=[pltpu.VMEM(((SEQ + FREQ) * ANSWER, LANES), jnp.float32)],
        compiler_params=pltpu.CompilerParams(vmem_limit_bytes=48 * MIB),
        name="inverse_blocks",
    )(spec, gate, wave)


def body(projected, live_blocks, filters, skip_gain):
    exchange = partial(lax.all_to_all, split_axis=0, concat_axis=0, tiled=True)
    wave = jnp.asarray(wave_tables())
    swap = ((0, 1), (1, 0))
    got = lax.ppermute(projected, "core", swap)
    got, gain = lax.optimization_barrier((got, lane_gains(skip_gain)))
    sent, gate = forward_blocks(live_blocks, projected, got, filters, wave)
    got_spec = exchange(sent.reshape(-1, 2, LANES), ("seq", "yh")).reshape(-1, LANES)
    mixed = mix_blocks(got_spec, gain)
    spec = exchange(mixed.reshape(-1, 2, LANES), "seq").reshape(-1, LANES)
    return inverse_blocks(spec, gate, wave)


def solution(mesh):
    split = Mesh(mesh.devices.reshape(SEQ, 2, 2), ("seq", "yh", "core"))
    chan = ("yh", "core")
    in_specs = (P(None, None, ("seq", "yh", "core")), P("seq"), P(chan, "seq"), P(chan))
    out_specs = P(chan, "seq")
    return jax.shard_map(body, mesh=split, in_specs=in_specs, out_specs=out_specs, check_vma=False)
```

```python
from functools import partial

import jax
import jax.numpy as jnp
import ml_dtypes
import numpy as np
from jax import lax
from jax.experimental import pallas as pl
from jax.experimental.pallas import tpu as pltpu
from jax.sharding import Mesh, PartitionSpec as P

BLOCK = 1024
SEQ = 128
CHAN = 4
GROUP = 16
FREQ = BLOCK // SEQ
LANES = 128
HALF = 64
SIGNAL = 4
MESSAGE = 6
PAIR = 2 * MESSAGE
ANSWER = FREQ + 2
MIB = 1024 * 1024
COST = pl.CostEstimate(flops=6_000_000_000, bytes_accessed=20_000_000, transcendentals=0)
ON_CHIP = pl.BlockSpec(memory_space=pltpu.VMEM)


BASE = BLOCK // 2
QUAD = FREQ // 2


def wave_tables():
    k = np.arange(BASE, dtype=np.int64).reshape(SEQ, QUAD).T.reshape(BASE, 1)
    t = np.arange(BLOCK, dtype=np.int64)[None, :]
    angle = 2.0 * np.pi * ((2 * k + 1) * t % (4 * BLOCK)) / (4 * BLOCK)
    return np.stack([np.cos(angle), -np.sin(angle)]).astype(ml_dtypes.bfloat16)


def lane_ids(shape):
    return lax.broadcasted_iota(jnp.int32, shape, len(shape) - 1)


def row_ids(shape):
    return lax.broadcasted_iota(jnp.int32, shape, len(shape) - 2)


def swap_parts(v):
    turned = pltpu.roll(v, HALF, 1)
    return jnp.where(lane_ids(v.shape) < HALF, -turned, turned)


SHIFTS = (2 * LANES, (CHAN - 1) * LANES)


def shift_kernel(out_ref):
    source, target = row_ids(SHIFTS), lane_ids(SHIFTS)
    place = source % HALF + GROUP * (target // LANES + 1) - jnp.where(source < LANES, 0, HALF)
    same_part = (source // HALF) % 2 == (target // HALF) % 2
    out_ref[...] = jnp.where(same_part & (place == target % HALF), 1.0, 0.0).astype(jnp.bfloat16)


def shift_matrix():
    return pl.pallas_call(
        shift_kernel,
        out_shape=jax.ShapeDtypeStruct(SHIFTS, jnp.bfloat16),
        out_specs=ON_CHIP,
        compiler_params=pltpu.CompilerParams(vmem_limit_bytes=48 * MIB),
        cost_estimate=COST,
        name="shift_matrix",
    )()


def gate_pieces(blk):
    return [(i, i % 2, blk * QUAD + i // 2) for i in range(BLOCK // LANES)]


def forward_kernel(
    live_ref, own_ref, got_ref, taps_ref, wave, out_ref, gate_ref, cols, packed, parcel
):
    high, core = lax.axis_index("yh"), lax.axis_index("core")
    lives = live_ref[...].astype(jnp.float32)
    places = lane_ids(lives.shape)
    side = 2 * GROUP
    piece = (GROUP, LANES)
    even = lane_ids(piece) % 2 == 0
    for part in range(2):
        rows = pl.ds(pl.multiple_of((2 * part + core) * GROUP, GROUP), GROUP)
        for blk in range(2):

            def read(i, at):
                return jnp.where(core == blk, own_ref[i, rows, at], got_ref[i, rows, at])

            to = part * HALF + blk * GROUP
            for block in range(BLOCK // LANES):
                at = pl.ds(block * LANES, LANES)
                number = (2 * high + blk) * (BLOCK // LANES) + block
                live = jnp.sum(jnp.where(places == number, lives, 0.0), axis=1, keepdims=True)
                key, value = read(1, at).astype(jnp.float32), read(2, at).astype(jnp.float32)
                value = key * value * live
                cols[pl.ds(to, GROUP), at] = value.astype(jnp.bfloat16)
                value = jnp.where(even, value, -value)
                cols[pl.ds(to + side, GROUP), at] = value.astype(jnp.bfloat16)
            gate = read(0, slice(None))

            @pl.when(high == part)
            def _():
                gate_ref[blk] = gate

            @pl.when(high != part)
            def _():
                for piece_at, row, number in gate_pieces(blk):
                    at = pl.ds(piece_at * LANES, LANES)
                    value = read(0, at).astype(jnp.float32)
                    parcel[row, pl.ds(number, GROUP, stride=FREQ), :] = value

    even = lane_ids((GROUP, BLOCK)) % 2 == 0
    taps = jnp.concatenate(
        [taps_ref[:, j * BLOCK : (j + 1) * BLOCK] for j in range(CHAN)], axis=0
    )
    top = taps.astype(jnp.bfloat16).astype(jnp.float32)
    taps = jnp.concatenate([top, taps - top, top, taps - top], axis=0)
    plain = even | (row_ids((GROUP, BLOCK)) < 2 * CHAN)
    cols[pl.ds(LANES, GROUP), :] = jnp.where(plain, taps, -taps).astype(jnp.bfloat16)
    cols[pl.ds(LANES + GROUP, LANES - GROUP), :] = jnp.zeros(
        (LANES - GROUP, BLOCK), jnp.bfloat16
    )
    weights = cols[...]
    sums = []
    for i in range(2):
        sums.append(
            lax.dot_general(
                wave[i], weights, (((1,), (1,)), ((), ())), preferred_element_type=jnp.float32
            )
        )

    def put(row, value):
        packed[pl.ds(row, SEQ, stride=PAIR), :] = value

    square = (SEQ, LANES)
    lane = lane_ids(square)
    comb = jnp.zeros(square, jnp.float32)
    for i in range(QUAD):
        at = slice(i * SEQ, (i + 1) * SEQ)
        cos, sin = sums[0][at, :LANES], sums[1][at, :LANES]
        sin = jnp.where(lane % HALF < side, sin, -sin)
        put(i, jnp.where(lane < HALF, cos, pltpu.roll(sin, HALF, 1)))
        put(MESSAGE + i, jnp.where(lane < HALF, pltpu.roll(cos, HALF, 1), sin))
        for part in range(2):
            move = part * HALF + i * GROUP
            value = sums[part][at, LANES:]
            comb = comb + (pltpu.roll(value, move, 1) if move else value)
    comb = jnp.where((lane >= HALF) & ((lane // (2 * CHAN)) % 2 == 1), -comb, comb)
    comb = comb + pltpu.roll(comb, LANES - CHAN, 1)
    top = comb.astype(jnp.bfloat16).astype(jnp.float32)
    comb = jnp.where((lane // CHAN) % 2 == 0, top, pltpu.roll(comb - top, CHAN, 1))
    for group in range(2):
        at = group * MESSAGE + SIGNAL
        put(at, jnp.where(high == group, comb, parcel[0, pl.ds(0, SEQ), :]))
        put(at + 1, jnp.where(high == group, 0.0, parcel[1, pl.ds(0, SEQ), :]))
    out_ref[...] = packed[pl.ds(0, SEQ * PAIR), :].astype(jnp.bfloat16)


def forward_blocks(live_blocks, own, got, taps, wave):
    gate = jax.ShapeDtypeStruct((2, GROUP, BLOCK), jnp.bfloat16)
    return pl.pallas_call(
        forward_kernel,
        out_shape=[jax.ShapeDtypeStruct((SEQ * PAIR, LANES), jnp.bfloat16), gate],
        in_specs=[ON_CHIP] * 5,
        out_specs=[ON_CHIP] * 2,
        scratch_shapes=[
            pltpu.VMEM((2 * LANES, BLOCK), jnp.bfloat16),
            pltpu.VMEM(((SEQ + 1) * PAIR, LANES), jnp.float32),
            pltpu.VMEM((2, SEQ + FREQ, LANES), jnp.float32),
        ],
        compiler_params=pltpu.CompilerParams(vmem_limit_bytes=48 * MIB),
        name="forward_blocks",
    )(live_blocks.reshape(1, -1), own, got, taps, wave)


def mix_kernel(in_ref, gain_ref, shift_ref, out_ref, spread, wide):
    spread[pl.ds(0, SEQ * PAIR), :] = in_ref[...].astype(jnp.float32)
    square = (SEQ, LANES)
    row, lane = row_ids(square), lane_ids(square)

    def take(at):
        return spread[pl.ds(at, SEQ, stride=PAIR), :]

    def put(row, value):
        wide[pl.ds(row, SEQ, stride=ANSWER), :] = value

    own = lax.axis_index("yh")
    extra = [take(at + SIGNAL) for at in (0, MESSAGE)]
    comb = jnp.where(own == 0, extra[0], extra[1])
    negate = jnp.where((row + lane) % SEQ == 0, 1.0, 0.0).astype(jnp.bfloat16)
    turned = jnp.dot(comb.T.astype(jnp.bfloat16), negate, preferred_element_type=jnp.float32)
    turned = turned + pltpu.roll(turned, LANES - CHAN, 0)
    late = jnp.where(lane == 0, 0.0, pltpu.roll(turned, SEQ - 1, 1))
    before = jnp.where(
        row % CHAN == 0, pltpu.roll(late, LANES - CHAN + 1, 0), pltpu.roll(turned, 1, 0)
    )
    half_row = row_ids((HALF, LANES))
    flip = (half_row // (4 * CHAN) + half_row // (2 * CHAN)) % 2 == 1
    before = jnp.where(jnp.concatenate([flip, flip], axis=0), -before, before)
    spec = (turned[:HALF] - before[HALF:], turned[HALF:] + before[:HALF])
    causal = lane <= row
    gain = jnp.concatenate([gain_ref[...]] * (LANES // GROUP), axis=1)
    low_lane = lane % HALF < 2 * GROUP
    signals, rows = [], []
    for k in range(FREQ):
        digit, mirror = k // 2, k % 2
        low, high = take(digit), take(MESSAGE + digit)
        if mirror == 0:
            signal = jnp.where(low_lane, low, pltpu.roll(high, 2 * GROUP, 1))
        else:
            signal = jnp.where(low_lane, pltpu.roll(low, LANES - 2 * GROUP, 1), high)
        late = jnp.where(row == 0, 0.0, pltpu.roll(signal, 1, 0))
        signals.append(signal)
        rows.append(jnp.concatenate([signal, late], axis=1).astype(jnp.bfloat16))
    rows = jnp.concatenate(rows, axis=0)
    moved = jnp.dot(rows, shift_ref[...], preferred_element_type=jnp.float32).astype(jnp.bfloat16)
    for k in range(FREQ):
        digit, mirror = k // 2, k % 2
        base = digit * 4 * CHAN + mirror * 2 * CHAN
        tiles = ([], [])
        for q in range(CHAN):
            for part in range(2):
                line = spec[part][base + q : base + q + 1, :]
                tall = jnp.broadcast_to(line, square)
                toeplitz = pltpu.roll(tall, 0, 1, stride=1, stride_axis=0)
                toeplitz = jnp.where(causal, toeplitz, 0.0)
                tiles[part].append(toeplitz.astype(jnp.bfloat16))
        signal = signals[k]
        at = slice(k * SEQ, (k + 1) * SEQ)
        shifted = [rows[at, :LANES]]
        shifted += [moved[at, q * LANES : (q + 1) * LANES] for q in range(CHAN - 1)]
        matrix = jnp.concatenate([jnp.concatenate(line, axis=1) for line in tiles], axis=0)
        parts = jnp.dot(
            matrix, jnp.concatenate(shifted, axis=0), preferred_element_type=jnp.float32
        )
        mixed = parts[:SEQ, :] + swap_parts(parts[SEQ:, :]) + gain * signal
        if mirror == 0:
            first = mixed
            continue
        plus, minus = first + mixed, first - mixed
        put(digit, jnp.where(lane < HALF, plus, minus))
        put(QUAD + digit, jnp.where(lane < HALF, minus, plus))
    put(FREQ, jnp.where(own == 0, extra[1], extra[0]))
    put(FREQ + 1, jnp.where(own == 0, take(PAIR - 1), take(MESSAGE - 1)))
    out_ref[...] = wide[pl.ds(0, SEQ * ANSWER), :].astype(jnp.bfloat16)


def mix_blocks(received, gain, shifts):
    return pl.pallas_call(
        mix_kernel,
        out_shape=jax.ShapeDtypeStruct((SEQ * ANSWER, LANES), jnp.bfloat16),
        in_specs=[ON_CHIP] * 3,
        out_specs=ON_CHIP,
        scratch_shapes=[
            pltpu.VMEM(((SEQ + 1) * PAIR, LANES), jnp.float32),
            pltpu.VMEM(((SEQ + 1) * ANSWER, LANES), jnp.float32),
        ],
        compiler_params=pltpu.CompilerParams(vmem_limit_bytes=48 * MIB),
        cost_estimate=COST,
        name="mix_blocks",
    )(received, gain, shifts)


def inverse_kernel(spec_ref, gate_ref, wave, out_ref, plain):
    plain[pl.ds(0, SEQ * ANSWER), :] = spec_ref[...].astype(jnp.float32)
    sides = [
        [plain[pl.ds(part * QUAD + i, SEQ, stride=ANSWER), :].T for i in range(QUAD)]
        for part in range(2)
    ]
    sides = [jnp.concatenate(side, axis=1).astype(jnp.bfloat16) for side in sides]
    total = None
    for part in range(2):
        lines = [side[part * HALF : (part + 1) * HALF, :] for side in sides]
        term = jnp.dot(
            jnp.concatenate(lines, axis=0), wave[part], preferred_element_type=jnp.float32
        )
        total = term if total is None else total + term
    high = lax.axis_index("yh")
    even = lane_ids((GROUP, BLOCK)) % 2 == 0
    for p in range(CHAN):
        at = p * GROUP
        value = jnp.where(
            even, total[at : at + GROUP, :], total[HALF + at : HALF + at + GROUP, :]
        )
        other = [
            plain[pl.ds(number * ANSWER + FREQ + row, GROUP, stride=FREQ * ANSWER), :]
            for _, row, number in gate_pieces(p % 2)
        ]
        other = jnp.concatenate(other, axis=1)
        gate = jnp.where(high == p // 2, gate_ref[p % 2].astype(jnp.float32), other)
        out_ref[:, pl.ds(p * BLOCK, BLOCK)] = (gate * (value * (1.0 / BLOCK))).astype(jnp.bfloat16)


def inverse_blocks(spec, gate, wave):
    return pl.pallas_call(
        inverse_kernel,
        out_shape=jax.ShapeDtypeStruct((GROUP, CHAN * BLOCK), jnp.bfloat16),
        in_specs=[ON_CHIP] * 3,
        out_specs=ON_CHIP,
        scratch_shapes=[pltpu.VMEM(((SEQ + FREQ) * ANSWER, LANES), jnp.float32)],
        compiler_params=pltpu.CompilerParams(vmem_limit_bytes=48 * MIB),
        name="inverse_blocks",
    )(spec, gate, wave)


def body(projected, live_blocks, filters, skip_gain):
    exchange = partial(lax.all_to_all, split_axis=0, concat_axis=0, tiled=True)
    wave = jnp.asarray(wave_tables())
    swap = ((0, 1), (1, 0))
    got = lax.ppermute(projected, "core", swap)
    got, shifts = lax.optimization_barrier((got, shift_matrix()))
    sent, gate = forward_blocks(live_blocks, projected, got, filters, wave)
    got_spec = exchange(sent.reshape(-1, 2, LANES), ("seq", "yh")).reshape(-1, LANES)
    mixed = mix_blocks(got_spec, skip_gain.reshape(1, GROUP), shifts)
    spec = exchange(mixed.reshape(-1, 2, LANES), "seq").reshape(-1, LANES)
    return inverse_blocks(spec, gate, wave)


def solution(mesh):
    split = Mesh(mesh.devices.reshape(SEQ, 2, 2), ("seq", "yh", "core"))
    chan = ("yh", "core")
    in_specs = (P(None, None, ("seq", "yh", "core")), P("seq"), P(chan, "seq"), P(chan))
    out_specs = P(chan, "seq")
    return jax.shard_map(body, mesh=split, in_specs=in_specs, out_specs=out_specs, check_vma=False)
```

```python
from functools import partial

import jax
import jax.numpy as jnp
import ml_dtypes
import numpy as np
from jax import lax
from jax.experimental import pallas as pl
from jax.experimental.pallas import tpu as pltpu
from jax.sharding import Mesh, PartitionSpec as P

BLOCK = 1024
SEQ = 128
CHAN = 4
GROUP = 16
FREQ = BLOCK // SEQ
LANES = 128
HALF = 64
SIGNAL = 4
MESSAGE = 6
PAIR = 2 * MESSAGE
ANSWER = FREQ + 2
MIB = 1024 * 1024
COST = pl.CostEstimate(flops=6_000_000_000, bytes_accessed=20_000_000, transcendentals=0)
ON_CHIP = pl.BlockSpec(memory_space=pltpu.VMEM)


BASE = BLOCK // 2
QUAD = FREQ // 2


def wave_tables():
    k = np.arange(BASE, dtype=np.int64).reshape(SEQ, QUAD).T.reshape(BASE, 1)
    t = np.arange(BLOCK, dtype=np.int64)[None, :]
    angle = 2.0 * np.pi * ((2 * k + 1) * t % (4 * BLOCK)) / (4 * BLOCK)
    return np.stack([np.cos(angle), -np.sin(angle)]).astype(ml_dtypes.bfloat16)


def lane_ids(shape):
    return lax.broadcasted_iota(jnp.int32, shape, len(shape) - 1)


def row_ids(shape):
    return lax.broadcasted_iota(jnp.int32, shape, len(shape) - 2)


def swap_parts(v):
    turned = pltpu.roll(v, HALF, 1)
    return jnp.where(lane_ids(v.shape) < HALF, -turned, turned)


def gain_kernel(gain_ref, out_ref):
    out_ref[...] = jnp.concatenate([gain_ref[...]] * (LANES // GROUP), axis=1)


def lane_gains(skip_gain):
    return pl.pallas_call(
        gain_kernel,
        out_shape=jax.ShapeDtypeStruct((1, LANES), jnp.float32),
        in_specs=[ON_CHIP],
        out_specs=ON_CHIP,
        compiler_params=pltpu.CompilerParams(vmem_limit_bytes=60 * MIB),
        cost_estimate=COST,
        name="lane_gains",
    )(skip_gain.reshape(1, GROUP))


def gate_pieces(blk):
    return [(i, i % 2, blk * QUAD + i // 2) for i in range(BLOCK // LANES)]


def forward_kernel(
    live_ref, own_ref, got_ref, taps_ref, wave, out_ref, gate_ref, cols, packed, parcel
):
    high, core = lax.axis_index("yh"), lax.axis_index("core")
    lives = live_ref[...].astype(jnp.float32)
    places = lane_ids(lives.shape)
    side = 2 * GROUP
    piece = (GROUP, LANES)
    even = lane_ids(piece) % 2 == 0
    for part in range(2):
        rows = pl.ds(pl.multiple_of((2 * part + core) * GROUP, GROUP), GROUP)
        for blk in range(2):

            def read(i, at):
                return jnp.where(core == blk, own_ref[i, rows, at], got_ref[i, rows, at])

            to = part * HALF + blk * GROUP
            for block in range(BLOCK // LANES):
                at = pl.ds(block * LANES, LANES)
                number = (2 * high + blk) * (BLOCK // LANES) + block
                live = jnp.sum(jnp.where(places == number, lives, 0.0), axis=1, keepdims=True)
                key, value = read(1, at).astype(jnp.float32), read(2, at).astype(jnp.float32)
                value = key * value * live
                cols[pl.ds(to, GROUP), at] = value.astype(jnp.bfloat16)
                value = jnp.where(even, value, -value)
                cols[pl.ds(to + side, GROUP), at] = value.astype(jnp.bfloat16)
            gate = read(0, slice(None))

            @pl.when(high == part)
            def _():
                gate_ref[blk] = gate

            @pl.when(high != part)
            def _():
                for piece_at, row, number in gate_pieces(blk):
                    at = pl.ds(piece_at * LANES, LANES)
                    value = read(0, at).astype(jnp.float32)
                    parcel[row, pl.ds(number, GROUP, stride=FREQ), :] = value

    even = lane_ids((GROUP, BLOCK)) % 2 == 0
    taps = jnp.concatenate(
        [taps_ref[:, j * BLOCK : (j + 1) * BLOCK] for j in range(CHAN)], axis=0
    )
    top = taps.astype(jnp.bfloat16).astype(jnp.float32)
    taps = jnp.concatenate([top, taps - top, top, taps - top], axis=0)
    plain = even | (row_ids((GROUP, BLOCK)) < 2 * CHAN)
    cols[pl.ds(LANES, GROUP), :] = jnp.where(plain, taps, -taps).astype(jnp.bfloat16)
    weights = cols[...]
    sums = []
    for i in range(2):
        sums.append(
            lax.dot_general(
                wave[i], weights, (((1,), (1,)), ((), ())), preferred_element_type=jnp.float32
            )
        )

    def put(row, value):
        packed[pl.ds(row, SEQ, stride=PAIR), :] = value

    square = (SEQ, LANES)
    lane = lane_ids(square)
    comb = jnp.zeros(square, jnp.float32)
    blank = jnp.zeros((SEQ, LANES - GROUP), jnp.float32)
    for i in range(QUAD):
        at = slice(i * SEQ, (i + 1) * SEQ)
        cos, sin = sums[0][at, :LANES], sums[1][at, :LANES]
        sin = jnp.where(lane % HALF < side, sin, -sin)
        put(i, jnp.where(lane < HALF, cos, pltpu.roll(sin, HALF, 1)))
        put(MESSAGE + i, jnp.where(lane < HALF, pltpu.roll(cos, HALF, 1), sin))
        for part in range(2):
            move = part * HALF + i * GROUP
            value = jnp.concatenate([sums[part][at, LANES:], blank], axis=1)
            comb = comb + (pltpu.roll(value, move, 1) if move else value)
    comb = jnp.where((lane >= HALF) & ((lane // (2 * CHAN)) % 2 == 1), -comb, comb)
    comb = comb + pltpu.roll(comb, LANES - CHAN, 1)
    top = comb.astype(jnp.bfloat16).astype(jnp.float32)
    comb = jnp.where((lane // CHAN) % 2 == 0, top, pltpu.roll(comb - top, CHAN, 1))
    for group in range(2):
        at = group * MESSAGE + SIGNAL
        put(at, jnp.where(high == group, comb, parcel[0, pl.ds(0, SEQ), :]))
        put(at + 1, jnp.where(high == group, 0.0, parcel[1, pl.ds(0, SEQ), :]))
    out_ref[...] = packed[pl.ds(0, SEQ * PAIR), :].astype(jnp.bfloat16)


def forward_blocks(live_blocks, own, got, taps, wave):
    gate = jax.ShapeDtypeStruct((2, GROUP, BLOCK), jnp.bfloat16)
    return pl.pallas_call(
        forward_kernel,
        out_shape=[jax.ShapeDtypeStruct((SEQ * PAIR, LANES), jnp.bfloat16), gate],
        in_specs=[ON_CHIP] * 5,
        out_specs=[ON_CHIP] * 2,
        scratch_shapes=[
            pltpu.VMEM((LANES + GROUP, BLOCK), jnp.bfloat16),
            pltpu.VMEM(((SEQ + 1) * PAIR, LANES), jnp.float32),
            pltpu.VMEM((2, SEQ + FREQ, LANES), jnp.float32),
        ],
        compiler_params=pltpu.CompilerParams(vmem_limit_bytes=48 * MIB),
        name="forward_blocks",
    )(live_blocks.reshape(1, -1), own, got, taps, wave)


def mix_kernel(in_ref, gain_ref, out_ref, spread, wide):
    spread[pl.ds(0, SEQ * PAIR), :] = in_ref[...].astype(jnp.float32)
    square = (SEQ, LANES)
    row, lane = row_ids(square), lane_ids(square)

    def take(at):
        return spread[pl.ds(at, SEQ, stride=PAIR), :]

    def put(row, value):
        wide[pl.ds(row, SEQ, stride=ANSWER), :] = value

    own = lax.axis_index("yh")
    extra = [take(at + SIGNAL) for at in (0, MESSAGE)]
    comb = jnp.where(own == 0, extra[0], extra[1])
    negate = jnp.where((row + lane) % SEQ == 0, 1.0, 0.0).astype(jnp.bfloat16)
    turned = jnp.dot(comb.T.astype(jnp.bfloat16), negate, preferred_element_type=jnp.float32)
    turned = turned + pltpu.roll(turned, LANES - CHAN, 0)
    late = jnp.where(lane == 0, 0.0, pltpu.roll(turned, SEQ - 1, 1))
    before = jnp.where(
        row % CHAN == 0, pltpu.roll(late, LANES - CHAN + 1, 0), pltpu.roll(turned, 1, 0)
    )
    half_row = row_ids((HALF, LANES))
    flip = (half_row // (4 * CHAN) + half_row // (2 * CHAN)) % 2 == 1
    before = jnp.where(jnp.concatenate([flip, flip], axis=0), -before, before)
    spec = (turned[:HALF] - before[HALF:], turned[HALF:] + before[:HALF])
    causal = lane <= row
    gain = gain_ref[...]
    low_lane = lane % HALF < 2 * GROUP
    signals, rows = [], []
    for k in range(FREQ):
        digit, mirror = k // 2, k % 2
        low, high = take(digit), take(MESSAGE + digit)
        if mirror == 0:
            signal = jnp.where(low_lane, low, pltpu.roll(high, 2 * GROUP, 1))
        else:
            signal = jnp.where(low_lane, pltpu.roll(low, LANES - 2 * GROUP, 1), high)
        late = jnp.where(row == 0, 0.0, pltpu.roll(signal, 1, 0))
        signals.append(signal)
        rows.append(jnp.concatenate([signal, late], axis=1).astype(jnp.bfloat16))
    rows = jnp.concatenate(rows, axis=0)
    shape = (2 * LANES, (CHAN - 1) * LANES)
    source, target = row_ids(shape), lane_ids(shape)
    place = source % HALF + GROUP * (target // LANES + 1) - jnp.where(source < LANES, 0, HALF)
    same_part = (source // HALF) % 2 == (target // HALF) % 2
    shifts = jnp.where(same_part & (place == target % HALF), 1.0, 0.0).astype(jnp.bfloat16)
    moved = jnp.dot(rows, shifts, preferred_element_type=jnp.float32).astype(jnp.bfloat16)
    for k in range(FREQ):
        digit, mirror = k // 2, k % 2
        base = digit * 4 * CHAN + mirror * 2 * CHAN
        tiles = ([], [])
        for q in range(CHAN):
            for part in range(2):
                line = spec[part][base + q : base + q + 1, :]
                tall = jnp.broadcast_to(line, square)
                toeplitz = pltpu.roll(tall, 0, 1, stride=1, stride_axis=0)
                toeplitz = jnp.where(causal, toeplitz, 0.0)
                tiles[part].append(toeplitz.astype(jnp.bfloat16))
        signal = signals[k]
        at = slice(k * SEQ, (k + 1) * SEQ)
        shifted = [rows[at, :LANES]]
        shifted += [moved[at, q * LANES : (q + 1) * LANES] for q in range(CHAN - 1)]
        matrix = jnp.concatenate([jnp.concatenate(line, axis=1) for line in tiles], axis=0)
        parts = jnp.dot(
            matrix, jnp.concatenate(shifted, axis=0), preferred_element_type=jnp.float32
        )
        mixed = parts[:SEQ, :] + swap_parts(parts[SEQ:, :]) + gain * signal
        if mirror == 0:
            first = mixed
            continue
        plus, minus = first + mixed, first - mixed
        put(digit, jnp.where(lane < HALF, plus, minus))
        put(QUAD + digit, jnp.where(lane < HALF, minus, plus))
    put(FREQ, jnp.where(own == 0, extra[1], extra[0]))
    put(FREQ + 1, jnp.where(own == 0, take(PAIR - 1), take(MESSAGE - 1)))
    out_ref[...] = wide[pl.ds(0, SEQ * ANSWER), :].astype(jnp.bfloat16)


def mix_blocks(received, gain):
    return pl.pallas_call(
        mix_kernel,
        out_shape=jax.ShapeDtypeStruct((SEQ * ANSWER, LANES), jnp.bfloat16),
        in_specs=[ON_CHIP, ON_CHIP],
        out_specs=ON_CHIP,
        scratch_shapes=[
            pltpu.VMEM(((SEQ + 1) * PAIR, LANES), jnp.float32),
            pltpu.VMEM(((SEQ + 1) * ANSWER, LANES), jnp.float32),
        ],
        compiler_params=pltpu.CompilerParams(vmem_limit_bytes=48 * MIB),
        cost_estimate=COST,
        name="mix_blocks",
    )(received, gain)


def inverse_kernel(spec_ref, gate_ref, wave, out_ref, plain):
    plain[pl.ds(0, SEQ * ANSWER), :] = spec_ref[...].astype(jnp.float32)
    sides = [
        [plain[pl.ds(part * QUAD + i, SEQ, stride=ANSWER), :].T for i in range(QUAD)]
        for part in range(2)
    ]
    sides = [jnp.concatenate(side, axis=1).astype(jnp.bfloat16) for side in sides]
    total = None
    for part in range(2):
        lines = [side[part * HALF : (part + 1) * HALF, :] for side in sides]
        term = jnp.dot(
            jnp.concatenate(lines, axis=0), wave[part], preferred_element_type=jnp.float32
        )
        total = term if total is None else total + term
    high = lax.axis_index("yh")
    even = lane_ids((GROUP, BLOCK)) % 2 == 0
    for p in range(CHAN):
        at = p * GROUP
        value = jnp.where(
            even, total[at : at + GROUP, :], total[HALF + at : HALF + at + GROUP, :]
        )
        other = [
            plain[pl.ds(number * ANSWER + FREQ + row, GROUP, stride=FREQ * ANSWER), :]
            for _, row, number in gate_pieces(p % 2)
        ]
        other = jnp.concatenate(other, axis=1)
        gate = jnp.where(high == p // 2, gate_ref[p % 2].astype(jnp.float32), other)
        out_ref[:, pl.ds(p * BLOCK, BLOCK)] = (gate * (value * (1.0 / BLOCK))).astype(jnp.bfloat16)


def inverse_blocks(spec, gate, wave):
    return pl.pallas_call(
        inverse_kernel,
        out_shape=jax.ShapeDtypeStruct((GROUP, CHAN * BLOCK), jnp.bfloat16),
        in_specs=[ON_CHIP] * 3,
        out_specs=ON_CHIP,
        scratch_shapes=[pltpu.VMEM(((SEQ + FREQ) * ANSWER, LANES), jnp.float32)],
        compiler_params=pltpu.CompilerParams(vmem_limit_bytes=48 * MIB),
        name="inverse_blocks",
    )(spec, gate, wave)


def body(projected, live_blocks, filters, skip_gain):
    exchange = partial(lax.all_to_all, split_axis=0, concat_axis=0, tiled=True)
    wave = jnp.asarray(wave_tables())
    swap = ((0, 1), (1, 0))
    got = lax.ppermute(projected, "core", swap)
    got, gain = lax.optimization_barrier((got, lane_gains(skip_gain)))
    sent, gate = forward_blocks(live_blocks, projected, got, filters, wave)
    got_spec = exchange(sent.reshape(-1, 2, LANES), ("seq", "yh")).reshape(-1, LANES)
    mixed = mix_blocks(got_spec, gain)
    spec = exchange(mixed.reshape(-1, 2, LANES), "seq").reshape(-1, LANES)
    return inverse_blocks(spec, gate, wave)


def solution(mesh):
    split = Mesh(mesh.devices.reshape(SEQ, 2, 2), ("seq", "yh", "core"))
    chan = ("yh", "core")
    in_specs = (P(None, None, ("seq", "yh", "core")), P("seq"), P(chan, "seq"), P(chan))
    out_specs = P(chan, "seq")
    return jax.shard_map(body, mesh=split, in_specs=in_specs, out_specs=out_specs, check_vma=False)
```

```python
from functools import partial

import jax
import jax.numpy as jnp
import ml_dtypes
import numpy as np
from jax import lax
from jax.experimental import pallas as pl
from jax.experimental.pallas import tpu as pltpu
from jax.sharding import Mesh, PartitionSpec as P

BLOCK = 1024
SEQ = 128
CHAN = 4
GROUP = 16
FREQ = BLOCK // SEQ
LANES = 128
HALF = 64
SIGNAL = 4
MESSAGE = 6
PAIR = 2 * MESSAGE
ANSWER = FREQ + 2
MIB = 1024 * 1024
COST = pl.CostEstimate(flops=6_000_000_000, bytes_accessed=20_000_000, transcendentals=0)
ON_CHIP = pl.BlockSpec(memory_space=pltpu.VMEM)


BASE = BLOCK // 2
QUAD = FREQ // 2


def wave_tables():
    k = np.arange(BASE, dtype=np.int64).reshape(SEQ, QUAD).T.reshape(BASE, 1)
    t = np.arange(BLOCK, dtype=np.int64)[None, :]
    angle = 2.0 * np.pi * ((2 * k + 1) * t % (4 * BLOCK)) / (4 * BLOCK)
    return np.stack([np.cos(angle), -np.sin(angle)]).astype(ml_dtypes.bfloat16)


def lane_ids(shape):
    return lax.broadcasted_iota(jnp.int32, shape, len(shape) - 1)


def row_ids(shape):
    return lax.broadcasted_iota(jnp.int32, shape, len(shape) - 2)


def swap_parts(v):
    turned = pltpu.roll(v, HALF, 1)
    return jnp.where(lane_ids(v.shape) < HALF, -turned, turned)


def gain_kernel(gain_ref, out_ref):
    out_ref[...] = jnp.concatenate([gain_ref[...]] * (LANES // GROUP), axis=1)


def lane_gains(skip_gain):
    return pl.pallas_call(
        gain_kernel,
        out_shape=jax.ShapeDtypeStruct((1, LANES), jnp.float32),
        in_specs=[ON_CHIP],
        out_specs=ON_CHIP,
        compiler_params=pltpu.CompilerParams(vmem_limit_bytes=60 * MIB),
        cost_estimate=COST,
        name="lane_gains",
    )(skip_gain.reshape(1, GROUP))


def gate_pieces(blk):
    return [(i, i % 2, blk * QUAD + i // 2) for i in range(BLOCK // LANES)]


def forward_kernel(
    live_ref, own_ref, got_ref, taps_ref, wave, out_ref, gate_ref, cols, packed, parcel
):
    high, core = lax.axis_index("yh"), lax.axis_index("core")
    lives = live_ref[...].astype(jnp.float32)
    places = lane_ids(lives.shape)
    side = 2 * GROUP
    piece = (GROUP, LANES)
    even = lane_ids(piece) % 2 == 0
    for part in range(2):
        rows = pl.ds(pl.multiple_of((2 * part + core) * GROUP, GROUP), GROUP)
        for blk in range(2):

            def read(i, at):
                return jnp.where(core == blk, own_ref[i, rows, at], got_ref[i, rows, at])

            to = part * HALF + blk * GROUP
            for block in range(BLOCK // LANES):
                at = pl.ds(block * LANES, LANES)
                number = (2 * high + blk) * (BLOCK // LANES) + block
                live = jnp.sum(jnp.where(places == number, lives, 0.0), axis=1, keepdims=True)
                key, value = read(1, at).astype(jnp.float32), read(2, at).astype(jnp.float32)
                value = key * value * live
                cols[pl.ds(to, GROUP), at] = value.astype(jnp.bfloat16)
                value = jnp.where(even, value, -value)
                cols[pl.ds(to + side, GROUP), at] = value.astype(jnp.bfloat16)
            gate = read(0, slice(None))

            @pl.when(high == part)
            def _():
                gate_ref[blk] = gate

            @pl.when(high != part)
            def _():
                for piece_at, row, number in gate_pieces(blk):
                    at = pl.ds(piece_at * LANES, LANES)
                    value = read(0, at).astype(jnp.float32)
                    parcel[row, pl.ds(number, GROUP, stride=FREQ), :] = value

    even = lane_ids((GROUP, BLOCK)) % 2 == 0
    taps = jnp.concatenate(
        [taps_ref[:, j * BLOCK : (j + 1) * BLOCK] for j in range(CHAN)], axis=0
    )
    top = taps.astype(jnp.bfloat16).astype(jnp.float32)
    taps = jnp.concatenate([top, taps - top, top, taps - top], axis=0)
    plain = even | (row_ids((GROUP, BLOCK)) < 2 * CHAN)
    cols[pl.ds(LANES, GROUP), :] = jnp.where(plain, taps, -taps).astype(jnp.bfloat16)
    cols[pl.ds(LANES + GROUP, LANES - GROUP), :] = jnp.zeros(
        (LANES - GROUP, BLOCK), jnp.bfloat16
    )
    weights = cols[...]
    sums = []
    for i in range(2):
        sums.append(
            lax.dot_general(
                wave[i], weights, (((1,), (1,)), ((), ())), preferred_element_type=jnp.float32
            )
        )

    def put(row, value):
        packed[pl.ds(row, SEQ, stride=PAIR), :] = value

    square = (SEQ, LANES)
    lane = lane_ids(square)
    comb = jnp.zeros(square, jnp.float32)
    for i in range(QUAD):
        at = slice(i * SEQ, (i + 1) * SEQ)
        cos, sin = sums[0][at, :LANES], sums[1][at, :LANES]
        sin = jnp.where(lane % HALF < side, sin, -sin)
        put(i, jnp.where(lane < HALF, cos, pltpu.roll(sin, HALF, 1)))
        put(MESSAGE + i, jnp.where(lane < HALF, pltpu.roll(cos, HALF, 1), sin))
        for part in range(2):
            move = part * HALF + i * GROUP
            value = sums[part][at, LANES:]
            comb = comb + (pltpu.roll(value, move, 1) if move else value)
    comb = jnp.where((lane >= HALF) & ((lane // (2 * CHAN)) % 2 == 1), -comb, comb)
    comb = comb + pltpu.roll(comb, LANES - CHAN, 1)
    top = comb.astype(jnp.bfloat16).astype(jnp.float32)
    comb = jnp.where((lane // CHAN) % 2 == 0, top, pltpu.roll(comb - top, CHAN, 1))
    for group in range(2):
        at = group * MESSAGE + SIGNAL
        put(at, jnp.where(high == group, comb, parcel[0, pl.ds(0, SEQ), :]))
        put(at + 1, jnp.where(high == group, 0.0, parcel[1, pl.ds(0, SEQ), :]))
    out_ref[...] = packed[pl.ds(0, SEQ * PAIR), :].astype(jnp.bfloat16)


def forward_blocks(live_blocks, own, got, taps, wave):
    gate = jax.ShapeDtypeStruct((2, GROUP, BLOCK), jnp.bfloat16)
    return pl.pallas_call(
        forward_kernel,
        out_shape=[jax.ShapeDtypeStruct((SEQ * PAIR, LANES), jnp.bfloat16), gate],
        in_specs=[ON_CHIP] * 5,
        out_specs=[ON_CHIP] * 2,
        scratch_shapes=[
            pltpu.VMEM((2 * LANES, BLOCK), jnp.bfloat16),
            pltpu.VMEM(((SEQ + 1) * PAIR, LANES), jnp.float32),
            pltpu.VMEM((2, SEQ + FREQ, LANES), jnp.float32),
        ],
        compiler_params=pltpu.CompilerParams(vmem_limit_bytes=48 * MIB),
        name="forward_blocks",
    )(live_blocks.reshape(1, -1), own, got, taps, wave)


def mix_kernel(in_ref, gain_ref, out_ref, spread, wide):
    spread[pl.ds(0, SEQ * PAIR), :] = in_ref[...].astype(jnp.float32)
    square = (SEQ, LANES)
    row, lane = row_ids(square), lane_ids(square)

    def take(at):
        return spread[pl.ds(at, SEQ, stride=PAIR), :]

    def put(row, value):
        wide[pl.ds(row, SEQ, stride=ANSWER), :] = value

    own = lax.axis_index("yh")
    extra = [take(at + SIGNAL) for at in (0, MESSAGE)]
    comb = jnp.where(own == 0, extra[0], extra[1])
    negate = jnp.where((row + lane) % SEQ == 0, 1.0, 0.0).astype(jnp.bfloat16)
    turned = jnp.dot(comb.T.astype(jnp.bfloat16), negate, preferred_element_type=jnp.float32)
    turned = turned + pltpu.roll(turned, LANES - CHAN, 0)
    late = jnp.where(lane == 0, 0.0, pltpu.roll(turned, SEQ - 1, 1))
    before = jnp.where(
        row % CHAN == 0, pltpu.roll(late, LANES - CHAN + 1, 0), pltpu.roll(turned, 1, 0)
    )
    half_row = row_ids((HALF, LANES))
    flip = (half_row // (4 * CHAN) + half_row // (2 * CHAN)) % 2 == 1
    before = jnp.where(jnp.concatenate([flip, flip], axis=0), -before, before)
    spec = (turned[:HALF] - before[HALF:], turned[HALF:] + before[:HALF])
    spec = [part * (1.0 / BLOCK) for part in spec]
    causal = lane <= row
    gain = gain_ref[...] * (1.0 / BLOCK)
    low_lane = lane % HALF < 2 * GROUP
    signals, rows = [], []
    for k in range(FREQ):
        digit, mirror = k // 2, k % 2
        low, high = take(digit), take(MESSAGE + digit)
        if mirror == 0:
            signal = jnp.where(low_lane, low, pltpu.roll(high, 2 * GROUP, 1))
        else:
            signal = jnp.where(low_lane, pltpu.roll(low, LANES - 2 * GROUP, 1), high)
        late = jnp.where(row == 0, 0.0, pltpu.roll(signal, 1, 0))
        signals.append(signal)
        rows.append(jnp.concatenate([signal, late], axis=1).astype(jnp.bfloat16))
    rows = jnp.concatenate(rows, axis=0)
    shape = (2 * LANES, (CHAN - 1) * LANES)
    source, target = row_ids(shape), lane_ids(shape)
    place = source % HALF + GROUP * (target // LANES + 1) - jnp.where(source < LANES, 0, HALF)
    same_part = (source // HALF) % 2 == (target // HALF) % 2
    shifts = jnp.where(same_part & (place == target % HALF), 1.0, 0.0).astype(jnp.bfloat16)
    moved = jnp.dot(rows, shifts, preferred_element_type=jnp.float32).astype(jnp.bfloat16)
    for k in range(FREQ):
        digit, mirror = k // 2, k % 2
        base = digit * 4 * CHAN + mirror * 2 * CHAN
        tiles = ([], [])
        for q in range(CHAN):
            for part in range(2):
                line = spec[part][base + q : base + q + 1, :]
                tall = jnp.broadcast_to(line, square)
                toeplitz = pltpu.roll(tall, 0, 1, stride=1, stride_axis=0)
                toeplitz = jnp.where(causal, toeplitz, 0.0)
                tiles[part].append(toeplitz.astype(jnp.bfloat16))
        signal = signals[k]
        at = slice(k * SEQ, (k + 1) * SEQ)
        shifted = [rows[at, :LANES]]
        shifted += [moved[at, q * LANES : (q + 1) * LANES] for q in range(CHAN - 1)]
        matrix = jnp.concatenate([jnp.concatenate(line, axis=1) for line in tiles], axis=0)
        parts = jnp.dot(
            matrix, jnp.concatenate(shifted, axis=0), preferred_element_type=jnp.float32
        )
        mixed = parts[:SEQ, :] + swap_parts(parts[SEQ:, :]) + gain * signal
        if mirror == 0:
            first = mixed
            continue
        plus, minus = first + mixed, first - mixed
        put(digit, jnp.where(lane < HALF, plus, minus))
        put(QUAD + digit, jnp.where(lane < HALF, minus, plus))
    put(FREQ, jnp.where(own == 0, extra[1], extra[0]))
    put(FREQ + 1, jnp.where(own == 0, take(PAIR - 1), take(MESSAGE - 1)))
    out_ref[...] = wide[pl.ds(0, SEQ * ANSWER), :].astype(jnp.bfloat16)


def mix_blocks(received, gain):
    return pl.pallas_call(
        mix_kernel,
        out_shape=jax.ShapeDtypeStruct((SEQ * ANSWER, LANES), jnp.bfloat16),
        in_specs=[ON_CHIP, ON_CHIP],
        out_specs=ON_CHIP,
        scratch_shapes=[
            pltpu.VMEM(((SEQ + 1) * PAIR, LANES), jnp.float32),
            pltpu.VMEM(((SEQ + 1) * ANSWER, LANES), jnp.float32),
        ],
        compiler_params=pltpu.CompilerParams(vmem_limit_bytes=48 * MIB),
        cost_estimate=COST,
        name="mix_blocks",
    )(received, gain)


def inverse_kernel(spec_ref, gate_ref, wave, out_ref, plain):
    plain[pl.ds(0, SEQ * ANSWER), :] = spec_ref[...].astype(jnp.float32)
    sides = [
        [plain[pl.ds(part * QUAD + i, SEQ, stride=ANSWER), :].T for i in range(QUAD)]
        for part in range(2)
    ]
    sides = [jnp.concatenate(side, axis=1).astype(jnp.bfloat16) for side in sides]
    total = None
    for part in range(2):
        lines = [side[part * HALF : (part + 1) * HALF, :] for side in sides]
        term = jnp.dot(
            jnp.concatenate(lines, axis=0), wave[part], preferred_element_type=jnp.float32
        )
        total = term if total is None else total + term
    high = lax.axis_index("yh")
    even = lane_ids((GROUP, BLOCK)) % 2 == 0
    for p in range(CHAN):
        at = p * GROUP
        value = jnp.where(
            even, total[at : at + GROUP, :], total[HALF + at : HALF + at + GROUP, :]
        )
        other = [
            plain[pl.ds(number * ANSWER + FREQ + row, GROUP, stride=FREQ * ANSWER), :]
            for _, row, number in gate_pieces(p % 2)
        ]
        other = jnp.concatenate(other, axis=1)
        gate = jnp.where(high == p // 2, gate_ref[p % 2].astype(jnp.float32), other)
        out_ref[:, pl.ds(p * BLOCK, BLOCK)] = (gate * value).astype(jnp.bfloat16)


def inverse_blocks(spec, gate, wave):
    return pl.pallas_call(
        inverse_kernel,
        out_shape=jax.ShapeDtypeStruct((GROUP, CHAN * BLOCK), jnp.bfloat16),
        in_specs=[ON_CHIP] * 3,
        out_specs=ON_CHIP,
        scratch_shapes=[pltpu.VMEM(((SEQ + FREQ) * ANSWER, LANES), jnp.float32)],
        compiler_params=pltpu.CompilerParams(vmem_limit_bytes=48 * MIB),
        name="inverse_blocks",
    )(spec, gate, wave)


def body(projected, live_blocks, filters, skip_gain):
    exchange = partial(lax.all_to_all, split_axis=0, concat_axis=0, tiled=True)
    wave = jnp.asarray(wave_tables())
    swap = ((0, 1), (1, 0))
    got = lax.ppermute(projected, "core", swap)
    got, gain = lax.optimization_barrier((got, lane_gains(skip_gain)))
    sent, gate = forward_blocks(live_blocks, projected, got, filters, wave)
    got_spec = exchange(sent.reshape(-1, 2, LANES), ("seq", "yh")).reshape(-1, LANES)
    mixed = mix_blocks(got_spec, gain)
    spec = exchange(mixed.reshape(-1, 2, LANES), "seq").reshape(-1, LANES)
    return inverse_blocks(spec, gate, wave)


def solution(mesh):
    split = Mesh(mesh.devices.reshape(SEQ, 2, 2), ("seq", "yh", "core"))
    chan = ("yh", "core")
    in_specs = (P(None, None, ("seq", "yh", "core")), P("seq"), P(chan, "seq"), P(chan))
    out_specs = P(chan, "seq")
    return jax.shard_map(body, mesh=split, in_specs=in_specs, out_specs=out_specs, check_vma=False)
```
